256 devices in a mesh: level: 4 (over x), wide: 64 (over y, z, core).
Axes of the slice: x: 4, y: 4, z: 8, core: 2. Of those that a mesh axis runs over, the one named last changes fastest.
Arguments:
- coarse_input: bfloat16 [256, 51200], P('wide', 'level'), may hold values from -6 to 6
- fine_input: bfloat16 [4, 128, 32768], P('level', 'wide'), may hold values from -6 to 6
- coarse_cotangent: float32 [256, 12800], P('wide', 'level'), may hold values from -6 to 6
- fine_cotangent: float32 [4, 128, 8192], P('level', 'wide'), may hold values from -6 to 6
- well_x: int32 [4], replicated, may hold values from 0 to 192
- well_y: int32 [4], replicated, may hold values from 0 to 24
- coarse_lift: bfloat16 [4, 48], replicated, may hold values from -3 to 3
- coarse_mixing: bfloat16 [48, 48], replicated, may hold values from -0.875 to 0.875
- coarse_spectral: bfloat16 [512, 32, 2, 2304], P(('level', 'wide')), may hold values from -8 to 8
- coarse_readout: bfloat16 [48], replicated, may hold values from -2 to 2
- fine_lift: bfloat16 [4, 5, 48], P('level'), may hold values from -2.5 to 2.5
- fine_mixing: bfloat16 [4, 48, 48], P('level'), may hold values from -0.875 to 0.875
- fine_spectral: bfloat16 [4, 512, 32, 2, 2304], P('level', 'wide'), may hold values from -6 to 6
- fine_readout: bfloat16 [4, 48], P('level'), may hold values from -2 to 2
Outputs:
- coarse_pred: bfloat16 [256, 12800], P('wide', 'level')
- fine_pred: bfloat16 [4, 128, 8192], P('level', 'wide')
- coarse_grad: float32 [512, 32, 2, 2304], P(('level', 'wide'))
- fine_grad: float32 [4, 512, 32, 2, 2304], P('level', 'wide')
The draws below stay inside these ranges and needn't reach their ends.
Inputs may be any that keep to these rules, and one draw needn't show every extreme that they name: Level l's box covers 128 // 2 global planes from well_x[l] on. Level l's box covers 128 // 2 global rows from 8 well_y[l] on.
All inputs are finite; a program needn't handle non-finite values.
Results may differ from the reference program's by a relative error of at most 0.014.
Values may be sent and summed in bfloat16 or wider, within the bound.
A program may use at most 128 MiB of HBM per device.

```python
import math
import jax
import jax.numpy as jnp
from jax import lax

C = 48
MODES = 16
CIN = 4
GX = 256
GY = 256
GZ = 50
FX = 128
FY = 128
FZ = 64
YB = 8
LEVELS = 4
KX2 = 32
KYZ = 512
CC = 2304


def touch_ends(drawn, rng, least, high):
    dims = drawn.shape
    index_at = [jax.random.randint(jax.random.fold_in(rng, axis), (), 0, dims[axis]) for axis in range(len(dims))]
    drawn = drawn.at[tuple(index_at)].set(least)
    longest = dims.index(max(dims))
    index_at[longest] = (index_at[longest] + 1) % dims[longest]
    return drawn.at[tuple(index_at)].set(high)


def shard_levels(own_key, extent, cuts, smallest, largest):
    def one(position, blocks):
        heights = jax.random.uniform(jax.random.fold_in(jax.random.fold_in(own_key, 6), position), (blocks,), jnp.float32, smallest / len(cuts), largest / len(cuts))
        return jnp.repeat(jnp.exp(heights), extent[position] // blocks).reshape((-1,) + (1,) * (len(extent) - position - 1))

    factor_of = one(*cuts[0])
    for cut in cuts[1:]:
        factor_of = factor_of * one(*cut)
    return factor_of


def gaussian(stream_key, shape, scale, reach, cuts=(), kind=jnp.bfloat16):
    entries = jax.random.normal(stream_key, shape, jnp.float32) * scale
    if len(cuts) > 0:
        entries = shard_levels(stream_key, shape, cuts, -0.22, 0.18) * entries
    return jnp.clip(entries, min=-reach, max=reach).astype(kind)


def setup_inputs(seed: int = 0) -> dict:
    key_list = jax.random.split(jax.random.key(seed), 15)
    coarse_input = gaussian(key_list[0], (GX, GY * GZ * CIN), 1.0, 6.0, ((0, 64), (1, 4)))
    fine_input = gaussian(key_list[1], (LEVELS, FX, FY * FZ * CIN), 1.0, 6.0, ((0, 4), (1, 64)))
    coarse_cotangent = gaussian(key_list[2], (GX, GY * GZ), 1.0, 6.0, ((0, 64), (1, 4)), jnp.float32)
    fine_cotangent = gaussian(key_list[3], (LEVELS, FX, FY * FZ), 1.0, 6.0, ((0, 4), (1, 64)), jnp.float32)
    well_x = touch_ends(jax.random.randint(key_list[4], (LEVELS,), 0, GX - FX // 2 + 1), jax.random.fold_in(key_list[4], 1), 0, (GX - FX // 2 + 1) - 1).astype(jnp.int32)
    well_y = touch_ends(jax.random.randint(key_list[5], (LEVELS,), 0, GY // YB - FY // 2 // YB + 1), jax.random.fold_in(key_list[5], 1), 0, (GY // YB - FY // 2 // YB + 1) - 1).astype(jnp.int32)
    coarse_lift = gaussian(key_list[6], (CIN, C), CIN ** -0.5, 3.0)
    coarse_mixing = gaussian(key_list[7], (C, C), C ** -0.5, 0.875)
    coarse_spectral = gaussian(key_list[8], (KYZ, KX2, 2, CC), 1.4, 8.0, ((0, 256),))
    coarse_readout = gaussian(key_list[9], (C,), 0.3, 2.0)
    fine_lift = gaussian(key_list[10], (LEVELS, CIN + 1, C), (CIN + 1) ** -0.5, 2.5, ((0, 4),))
    fine_mixing = gaussian(key_list[11], (LEVELS, C, C), C ** -0.5, 0.875, ((0, 4),))
    fine_spectral = gaussian(key_list[12], (LEVELS, KYZ, KX2, 2, CC), 0.8, 6.0, ((0, 4), (1, 64)))
    fine_readout = gaussian(key_list[13], (LEVELS, C), 0.3, 2.0, ((0, 4),))
    return {"coarse_input": coarse_input, "fine_input": fine_input, "coarse_cotangent": coarse_cotangent, "fine_cotangent": fine_cotangent, "well_x": well_x, "well_y": well_y, "coarse_lift": coarse_lift, "coarse_mixing": coarse_mixing, "coarse_spectral": coarse_spectral, "coarse_readout": coarse_readout, "fine_lift": fine_lift, "fine_mixing": fine_mixing, "fine_spectral": fine_spectral, "fine_readout": fine_readout}


HIGH = lax.Precision.HIGHEST

def waves(row_ids, freq_ids, length):
    signed = jnp.where(freq_ids < MODES, freq_ids, freq_ids - 2 * MODES)
    product = jnp.mod(row_ids[:, None] * signed[None, :], length)
    angles = product.astype(jnp.float32) * (2.0 * math.pi / length)
    factor = 1.0 / math.sqrt(length)
    return (jnp.cos(angles) * factor, jnp.sin(angles) * factor)

def depth_table(length):
    cosine, sine_part = waves(jnp.arange(length, dtype=jnp.int32), jnp.arange(MODES, dtype=jnp.int32), length)
    return jnp.concatenate([cosine, -sine_part], axis=1)

def along_y(spectra, cosine, sine_part):
    real_part = spectra[:, :, :MODES]
    imag_part = spectra[:, :, MODES:]
    out_real = jnp.einsum('xykc,yj->jkxc', real_part, cosine, precision=HIGH) + jnp.einsum('xykc,yj->jkxc', imag_part, sine_part, precision=HIGH)
    out_imag = jnp.einsum('xykc,yj->jkxc', imag_part, cosine, precision=HIGH) - jnp.einsum('xykc,yj->jkxc', real_part, sine_part, precision=HIGH)
    return jnp.stack([out_real, out_imag], axis=3)

def back_y(pieces, cosine, sine_part):
    real_part = pieces[:, :, :, 0]
    imag_part = pieces[:, :, :, 1]
    out_real = jnp.einsum('jkxc,yj->xykc', real_part, cosine, precision=HIGH) - jnp.einsum('jkxc,yj->xykc', imag_part, sine_part, precision=HIGH)
    out_imag = jnp.einsum('jkxc,yj->xykc', imag_part, cosine, precision=HIGH) + jnp.einsum('jkxc,yj->xykc', real_part, sine_part, precision=HIGH)
    return jnp.concatenate([out_real, out_imag], axis=2)

def along_x(blocks):
    length = blocks.shape[1]
    cosine, sine_part = waves(jnp.arange(length, dtype=jnp.int32), jnp.arange(2 * MODES, dtype=jnp.int32), length)
    real_part = blocks[:, :, 0]
    imag_part = blocks[:, :, 1]
    out_real = jnp.einsum('mxc,xj->mjc', real_part, cosine, precision=HIGH) + jnp.einsum('mxc,xj->mjc', imag_part, sine_part, precision=HIGH)
    out_imag = jnp.einsum('mxc,xj->mjc', imag_part, cosine, precision=HIGH) - jnp.einsum('mxc,xj->mjc', real_part, sine_part, precision=HIGH)
    return jnp.stack([out_real, out_imag], axis=2)

def back_x(spectra, length):
    cosine, sine_part = waves(jnp.arange(length, dtype=jnp.int32), jnp.arange(2 * MODES, dtype=jnp.int32), length)
    real_part = spectra[:, :, 0]
    imag_part = spectra[:, :, 1]
    out_real = jnp.einsum('mjc,xj->mxc', real_part, cosine, precision=HIGH) - jnp.einsum('mjc,xj->mxc', imag_part, sine_part, precision=HIGH)
    out_imag = jnp.einsum('mjc,xj->mxc', imag_part, cosine, precision=HIGH) + jnp.einsum('mjc,xj->mxc', real_part, sine_part, precision=HIGH)
    return jnp.stack([out_real, out_imag], axis=2)

def mixed(spectra, weights):
    real_part = spectra[:, :, 0]
    imag_part = spectra[:, :, 1]
    weight_real = weights[:, :, 0]
    weight_imag = weights[:, :, 1]
    out_real = jnp.einsum('mjc,mjcd->mjd', real_part, weight_real, precision=HIGH) - jnp.einsum('mjc,mjcd->mjd', imag_part, weight_imag, precision=HIGH)
    out_imag = jnp.einsum('mjc,mjcd->mjd', real_part, weight_imag, precision=HIGH) + jnp.einsum('mjc,mjcd->mjd', imag_part, weight_real, precision=HIGH)
    return jnp.stack([out_real, out_imag], axis=2)

def mixed_adjoint(spectra, weights):
    real_part = spectra[:, :, 0]
    imag_part = spectra[:, :, 1]
    weight_real = weights[:, :, 0]
    weight_imag = weights[:, :, 1]
    out_real = jnp.einsum('mjd,mjcd->mjc', real_part, weight_real, precision=HIGH) + jnp.einsum('mjd,mjcd->mjc', imag_part, weight_imag, precision=HIGH)
    out_imag = jnp.einsum('mjd,mjcd->mjc', imag_part, weight_real, precision=HIGH) - jnp.einsum('mjd,mjcd->mjc', real_part, weight_imag, precision=HIGH)
    return jnp.stack([out_real, out_imag], axis=2)

def weight_grads(source, target):
    source_real = source[:, :, 0]
    source_imag = source[:, :, 1]
    target_real = target[:, :, 0]
    target_imag = target[:, :, 1]
    grad_real = jnp.einsum('mjc,mjd->mjcd', source_real, target_real, precision=HIGH) + jnp.einsum('mjc,mjd->mjcd', source_imag, target_imag, precision=HIGH)
    grad_imag = jnp.einsum('mjc,mjd->mjcd', source_real, target_imag, precision=HIGH) - jnp.einsum('mjc,mjd->mjcd', source_imag, target_real, precision=HIGH)
    stacked = jnp.stack([grad_real, grad_imag], axis=2)
    return stacked.reshape(stacked.shape[0], stacked.shape[1], 2, stacked.shape[3] * stacked.shape[4])

def rounded(values):
    return lax.optimization_barrier(values.astype(jnp.bfloat16))

def reference(coarse_input, fine_input, coarse_cotangent, fine_cotangent, well_x, well_y, coarse_lift, coarse_mixing, coarse_spectral, coarse_readout, fine_lift, fine_mixing, fine_spectral, fine_readout):
    coarse_table = depth_table(GZ)
    coarse_bf = coarse_table.astype(jnp.bfloat16).astype(jnp.float32)
    row_cos, row_sin = waves(jnp.arange(GY, dtype=jnp.int32), jnp.arange(2 * MODES, dtype=jnp.int32), GY)
    planes_in = coarse_input.reshape(GX, GY, GZ, CIN)
    lift_g = coarse_lift.astype(jnp.float32)
    mixing_g = coarse_mixing.astype(jnp.float32)
    readout_g = coarse_readout.astype(jnp.float32)

    def lift_plane(plane_in):
        return rounded(jnp.einsum('yzi,ic->yzc', plane_in.astype(jnp.float32), lift_g, precision=HIGH))

    def plane_modes(grid_field):
        spectra = jnp.einsum('yzc,zk->ykc', grid_field.astype(jnp.float32), coarse_bf, precision=HIGH)[None]
        return along_y(spectra, row_cos, row_sin).reshape(2 * MODES * MODES, 2, C)
    plane_spectra = lax.map(lambda plane_in: plane_modes(lift_plane(plane_in)), planes_in)
    coarse_modes = along_x(jnp.transpose(plane_spectra, (1, 0, 2, 3)))
    coarse_weights = coarse_spectral.astype(jnp.float32).reshape(KYZ, KX2, 2, C, C)
    returned = jnp.transpose(back_x(mixed(coarse_modes, coarse_weights), GX), (1, 0, 2, 3))

    def plane_pre(plane_in, column):
        lifted = lift_plane(plane_in).astype(jnp.float32)
        spectral = back_y(column.reshape(2 * MODES, MODES, 1, 2, C), row_cos, row_sin)[0]
        spectral = rounded(spectral).astype(jnp.float32)
        return jnp.einsum('ykc,zk->yzc', spectral, coarse_bf, precision=HIGH) + jnp.einsum('yzc,cd->yzd', lifted, mixing_g, precision=HIGH)

    def plane_out(inputs_pair):
        pre_values = plane_pre(inputs_pair[0], inputs_pair[1])
        hidden = rounded(jax.nn.gelu(pre_values)).astype(jnp.float32)
        return jnp.einsum('yzc,c->yz', hidden, readout_g, precision=HIGH).astype(jnp.bfloat16)
    coarse_pred = lax.map(plane_out, (planes_in, returned))
    fine_table = depth_table(FZ)
    fine_bf = fine_table.astype(jnp.bfloat16).astype(jnp.float32)
    fine_cos, fine_sin = waves(jnp.arange(FY, dtype=jnp.int32), jnp.arange(2 * MODES, dtype=jnp.int32), FY)
    depth_map = ((jnp.arange(FZ, dtype=jnp.int32) * GZ // FZ)[None, :] == jnp.arange(GZ, dtype=jnp.int32)[:, None]).astype(jnp.float32)

    def fine_forward(grid_field):
        spectra = jnp.einsum('xyzc,zk->xykc', grid_field.astype(jnp.float32), fine_bf, precision=HIGH)
        return along_x(along_y(spectra, fine_cos, fine_sin).reshape(2 * MODES * MODES, FX, 2, C))

    def fine_inverse(spectra):
        columns = back_x(spectra, FX).reshape(2 * MODES, MODES, FX, 2, C)
        spectral = rounded(back_y(columns, fine_cos, fine_sin)).astype(jnp.float32)
        return jnp.einsum('xykc,zk->xyzc', spectral, fine_bf, precision=HIGH)
    coarse_back = coarse_cotangent.reshape(GX, GY, GZ)
    fine_preds = []
    fine_grads = []
    for level_id in range(LEVELS):
        start_x = well_x[level_id].astype(jnp.int32)
        start_y = (well_y[level_id] * YB).astype(jnp.int32)
        start_z = jnp.zeros((), jnp.int32)
        box = lax.dynamic_slice(coarse_pred, (start_x, start_y, start_z), (FX // 2, FY // 2, GZ))
        refined = jnp.einsum('xyg,gf->xyf', box.astype(jnp.float32), depth_map, precision=HIGH).astype(jnp.bfloat16)
        refined = jnp.repeat(jnp.repeat(refined, 2, axis=0), 2, axis=1)
        features = fine_input[level_id].reshape(FX, FY, FZ, CIN)
        stacked = jnp.concatenate([features, refined[..., None]], axis=3)
        lift_f = fine_lift[level_id].astype(jnp.float32)
        mixing_f = fine_mixing[level_id].astype(jnp.float32)
        readout_f = fine_readout[level_id].astype(jnp.float32)
        lifted = rounded(jnp.einsum('xyzi,ic->xyzc', stacked.astype(jnp.float32), lift_f, precision=HIGH))
        weights_f = fine_spectral[level_id].astype(jnp.float32).reshape(KYZ, KX2, 2, C, C)
        fine_modes = fine_forward(lifted)
        pre_values = fine_inverse(mixed(fine_modes, weights_f)) + jnp.einsum('xyzc,cd->xyzd', lifted.astype(jnp.float32), mixing_f, precision=HIGH)
        hidden, slope = jax.vjp(jax.nn.gelu, pre_values)
        hidden_b = rounded(hidden).astype(jnp.float32)
        fine_preds.append(jnp.einsum('xyzc,c->xyz', hidden_b, readout_f, precision=HIGH).astype(jnp.bfloat16).reshape(FX, FY * FZ))
        pull = fine_cotangent[level_id].reshape(FX, FY, FZ)[..., None] * readout_f
        push = rounded(slope(pull)[0])
        dual = fine_forward(push)
        fine_grads.append(weight_grads(fine_modes, dual))
        back_field = fine_inverse(mixed_adjoint(dual, weights_f)) + jnp.einsum('xyzd,cd->xyzc', push.astype(jnp.float32), mixing_f, precision=HIGH)
        coarse_part = jnp.einsum('xyzc,c->xyz', back_field, lift_f[CIN], precision=HIGH)
        pooled = coarse_part.reshape(FX // 2, 2, FY // 2, 2, FZ).sum(axis=(1, 3))
        pooled = jnp.einsum('xyf,gf->xyg', pooled, depth_map, precision=HIGH)
        current = lax.dynamic_slice(coarse_back, (start_x, start_y, start_z), (FX // 2, FY // 2, GZ))
        coarse_back = lax.dynamic_update_slice(coarse_back, current + pooled, (start_x, start_y, start_z))

    def plane_back(inputs_triple):
        pre_values = plane_pre(inputs_triple[0], inputs_triple[1])
        hidden, slope = jax.vjp(jax.nn.gelu, pre_values)
        push = rounded(slope(inputs_triple[2][..., None] * readout_g)[0])
        return plane_modes(push)
    dual_planes = lax.map(plane_back, (planes_in, returned, coarse_back))
    coarse_dual = along_x(jnp.transpose(dual_planes, (1, 0, 2, 3)))
    coarse_grad = weight_grads(coarse_modes, coarse_dual)
    return (coarse_pred.reshape(GX, GY * GZ), jnp.stack(fine_preds, axis=0), coarse_grad, jnp.stack(fine_grads, axis=0))
```

```python
import math

import ml_dtypes
import numpy as np
import jax
import jax.numpy as jnp
from jax import lax
from jax.experimental import pallas as pl
from jax.experimental.pallas import tpu as pltpu
from jax.sharding import PartitionSpec as P

MODES = 16
KF = 2 * MODES
CH = 48
NB = 6
CL = 8
GX = 256
GY = 256
GZ = 50
FX = 128
FY = 128
FZ = 64
ZP = 64
LV = 4
WD = 64
PG = 4
YG = 64
PF = 2
CC = CH * CH
BF = jnp.bfloat16
F32 = jnp.float32
HIGH = lax.Precision.HIGHEST
VMEM_BYTES = 48 * 2**20


def bf(x):
    return np.asarray(x, np.float32).astype(ml_dtypes.bfloat16)


def f32(x):
    return np.asarray(x, np.float32)


def waves(rows, length):
    j = np.arange(KF)
    signed = np.where(j < MODES, j, j - KF)
    turn = np.mod(rows[:, None] * signed[None, :], length) * (2.0 * math.pi / length)
    return np.cos(turn) / math.sqrt(length), np.sin(turn) / math.sqrt(length)


def forward_table(rows, length):
    c, s = waves(rows, length)
    c, s = c.T, s.T
    return np.stack([np.stack([c, s], 1), np.stack([-s, c], 1)], 0)


def depth(length):
    c, s = waves(np.arange(length), length)
    both = np.stack([c[:, :MODES], -s[:, :MODES]], 1)
    both = bf(both).astype(np.float64)
    return np.concatenate([both, np.zeros((ZP - length, 2, MODES))], 0)


D_G, D_F = depth(GZ), depth(FZ)
ZMAP = np.zeros((ZP, FZ))
ZMAP[np.arange(FZ) * GZ // FZ, np.arange(FZ)] = 1.0
D_POOL = np.einsum("gf,frk->grk", ZMAP, D_F)


def depth_blocks(d):
    return np.einsum("zrk,ij->zirkj", d, np.eye(CL)).reshape(ZP * CL, 2 * MODES * CL)


def depth_features(d, length):
    return np.einsum("zrk,ij->zirkj", d[:length], np.eye(4)).reshape(length * 4, 2 * MODES * 4)


ZF_G, ZF_F = bf(depth_blocks(D_G)), bf(depth_blocks(D_F))
ZI_G, ZI_F = bf(depth_blocks(D_G).T), bf(depth_blocks(D_F).T)
Z4_G, Z4_F = bf(depth_features(D_G, GZ)), bf(depth_features(D_F, FZ))
ZC = f32(D_POOL.reshape(ZP, 2 * MODES))

FY_G = np.stack([forward_table(v * YG + np.arange(YG), GY) for v in range(LV)], 0)
FY_F = forward_table(np.arange(FY), FY)
FY_BOX = FY_F.reshape(2, KF, 2, FY // 2, 2).sum(4)
FX_G = forward_table(np.arange(GX), GX)
FX_F = forward_table(np.arange(FX), FX)
FX_BOX = FX_F.reshape(2, KF, 2, FX // 2, 2).sum(4)
EYE_G, EYE_F = np.eye(PG), np.eye(PF)

TYA_G = f32(np.einsum("vakbt,pq->vakpbtq", FY_G, EYE_G).reshape(LV, 2 * KF * PG, 2 * YG * PG))
TYA_F = f32(np.einsum("akbt,pq->akpbtq", FY_F, EYE_F).reshape(2 * KF * PF, 2 * FY * PF))
TYA_BOX = f32(np.einsum("akbt,pq->akpbtq", FY_BOX, EYE_G).reshape(2 * KF * PG, FY * PG))
TYF_G = bf(np.einsum("vakbt,pq->vkpabtq", FY_G, EYE_G).reshape(LV, KF * PG * 2, 2 * YG * PG))
TYF_F = bf(np.einsum("akbt,pq->kpabtq", FY_F, EYE_F).reshape(KF * PF * 2, 2 * FY * PF))
TYI_G = bf(np.einsum("vbkat,pq->vatpkqb", FY_G, EYE_G).reshape(LV, 2 * YG * PG, KF * PG * 2))
TYI_F = bf(np.einsum("bkat,pq->atpkqb", FY_F, EYE_F).reshape(2 * FY * PF, KF * PF * 2))
TYB_BOX = np.zeros((4, 448, 2 * KF), np.float32)
TYB_BOX[:, 192:256] = np.repeat(FY_BOX.transpose(2, 0, 3, 1).reshape(4, FY // 2, KF), 2, axis=2)
DD_BOX = bf(np.einsum("zahk,pq,rs->hprkasqz", D_POOL.reshape(ZP, 2, 2, 8), EYE_G, np.eye(2)).reshape(128, 4 * PG * ZP))


def source_rows(table):
    a = np.stack([table[0], -table[1]], 1)
    b = np.stack([table[1], table[0]], 1)
    return np.stack([a, b], 0).reshape(4 * KF, 2, -1)


def in_rows(table, planes, first):
    rows = source_rows(table).reshape(4 * KF, 2, WD, planes)
    out = np.zeros((4 * KF, 2, WD, 8))
    out[..., first : first + planes] = rows
    return out.reshape(4 * KF, 2 * WD * 8)


TXS_G = f32(in_rows(FX_G, PG, 0))
TXS_F = f32(in_rows(FX_F, PF, PG))
TXS_BOX = f32(source_rows(FX_BOX).reshape(4 * KF, FX))


def dual_rows(table, count):
    r, i = table[0], table[1]
    kinds = [np.stack([r, r], 1), np.stack([i, i], 1), np.stack([r, i], 1), np.stack([i, -r], 1)]
    rows = np.stack(kinds[:count], 0).transpose(0, 1, 2, 4, 3)
    return rows.reshape(count * 2 * KF, -1)


TXD_G = bf(dual_rows(FX_G, 2))
TXD_F = bf(dual_rows(FX_F, 4))


def back_rows(table):
    back = table.transpose(3, 2, 0, 1)
    back = np.stack([back, back], 4)
    return back.reshape(back.shape[0] * 2, 4 * KF)


TXB_G = bf(back_rows(FX_G))
TXB_F = bf(back_rows(FX_F))
TXB_BOX = f32(back_rows(FX_BOX))

PERM = np.zeros((MODES, NB, CL, NB, MODES, CL))
for _k in range(MODES):
    for _b in range(NB):
        for _l in range(CL):
            PERM[_k, _b, _l, _b, _k, _l] = 1.0
PERM = PERM.reshape(MODES * CH, MODES * CH)
PERM_IN, PERM_OUT = bf(PERM), bf(PERM.T)
PERM_WIDE = np.zeros((8, 128, MODES * CH))
PERM_WIDE[:, : 2 * CH] = PERM.reshape(8, 2 * CH, MODES * CH)
PERM_WIDE = bf(PERM_WIDE.reshape(1024, MODES * CH))
SPREAD_IN = bf(np.kron(np.eye(CH), np.ones((1, CH))))
SPREAD_OUT = bf(np.kron(np.ones((1, CH)), np.eye(CH)))
FOLD_IN = bf(np.kron(np.ones((CH, 1)), np.eye(CH)))
ONES_CL = bf(np.kron(np.eye(ZP), np.ones((1, CL))))
SUM_CL = bf(np.kron(np.eye(ZP), np.ones((CL, 1))))
TILE_CL = f32(np.kron(np.ones((1, ZP)), np.eye(CL)))
ROWS_UP = np.kron(np.eye(FY // 2), np.ones((2 * PF, 1))).reshape(256, FY // 4, 2).transpose(2, 0, 1)
ROWS_UP = bf(ROWS_UP)
ROWS_DOWN = f32(np.kron(np.eye(FY // 2), np.ones((1, 2 * PF))))
Z_UP = bf(ZMAP)
Z_DOWN = f32(ZMAP.T)


def mm(a, b):
    return jnp.dot(a, b, preferred_element_type=F32)


def mmh(a, b):
    return jnp.dot(a, b, preferred_element_type=F32, precision=HIGH)


MESH = pl.DeviceIdType.MESH
DMA2 = pltpu.SemaphoreType.DMA((2,))


def vm(shape, kind=F32):
    return pltpu.VMEM(shape, kind)


def run(body, outs, *args, meta=None, scratch=(), cid=None, name=None):
    specs = [pl.BlockSpec(memory_space=pltpu.VMEM)] * len(args)
    if meta is not None:
        specs = [pl.BlockSpec(memory_space=pltpu.SMEM)] + specs
        args = (meta,) + args
    return pl.pallas_call(
        body,
        out_shape=[jax.ShapeDtypeStruct(s, d) for s, d in outs],
        in_specs=specs,
        out_specs=[pl.BlockSpec(memory_space=pltpu.VMEM)] * len(outs),
        scratch_shapes=list(scratch),
        name=name,
        compiler_params=pltpu.CompilerParams(
            vmem_limit_bytes=VMEM_BYTES, collective_id=cid, has_side_effects=cid is not None),
    )(*args)


def features_body(rows, planes, width, x_ref, z_ref, t_ref, feat_ref, out_ref, scr, level=None):
    for y in range(rows):
        scr[planes * y : planes * (y + 1), :] = x_ref[:, width * y : width * (y + 1)].astype(F32)
    feat = scr[...].astype(BF)
    feat_ref[...] = feat
    a = mm(feat, z_ref[...])
    half = a.shape[1] // 2
    stacked = jnp.concatenate([a[:, :half], a[:, half:]], axis=0)
    both = mmh(t_ref[...] if level is None else t_ref[level], stacked)
    rows_out = both.shape[0] // 2
    lanes = jnp.concatenate([both[:rows_out], both[rows_out:]], axis=1)
    out_ref[...] = lanes.reshape(out_ref.shape)


def features_g_body(meta, x_ref, z_ref, t_ref, feat_ref, out_ref, scr):
    features_body(YG, PG, GZ * 4, x_ref, z_ref, t_ref, feat_ref, out_ref, scr, meta[0])


def features_f_body(x_ref, z_ref, t_ref, feat_ref, out_ref, scr):
    features_body(FY, PF, FZ * 4, x_ref, z_ref, t_ref, feat_ref, out_ref, scr)


def pair_rows(scr, first, stride, count):
    even = scr[pl.ds(first, count, stride=2 * stride), :]
    odd = scr[pl.ds(first + stride, count, stride=2 * stride), :]
    return jnp.concatenate([even, odd], axis=1)


def box_body(meta, rows_ref, z_ref, t_ref, spec_ref, planes_ref, rows_scr, box_scr, s_scr, o_scr):
    rows_scr[...] = rows_ref[...].astype(F32).reshape(rows_scr.shape)
    box = rows_scr[pl.ds(pl.multiple_of(meta[2] * PG, 32), 256), :]
    box_scr[...] = box
    for p in range(PG):
        planes_ref[lax.rem(p + GX - meta[1], PG)] = pair_rows(box_scr, p, PG, FY // 4).astype(BF)
    a = mmh(box, z_ref[...])
    s_scr[...] = mmh(t_ref[...], jnp.concatenate([a[:, :MODES], a[:, MODES:]], axis=0))
    for p in range(PG):
        for r in range(2):
            at = 2 * MODES * p + MODES * r
            o_scr[:, at : at + MODES] = s_scr[pl.ds(KF * PG * r + p, KF, stride=PG), :]
    spec_ref[...] = o_scr[...].reshape(spec_ref.shape)


def mix_modes(s, modes, w_ref, e_ref, r_ref, t_ref, put, extra=None):
    half = s.shape[0] // 2
    for m in range(modes):
        sa = s[:half, CH * m : CH * (m + 1)].astype(BF)
        sb = s[half:, CH * m : CH * (m + 1)].astype(BF)
        w = w_ref[m].reshape(half, CC).astype(F32)
        pa = mm((w * mm(sa, e_ref[...])).astype(BF), r_ref[...])
        pb = mm((w * mm(sb, e_ref[...])).astype(BF), r_ref[...])
        both = jnp.concatenate([pa, pb], axis=0).astype(BF)
        put(m, mm(t_ref[...], both))
        if extra is not None:
            extra(m, w)


def halves(u):
    half = u.shape[1] // 2
    return jnp.concatenate([u[:, :half], u[:, half:]], axis=0)


def selector(lift_ref, count, first):
    rows = lax.broadcasted_iota(jnp.int32, (MODES * 4, count * CH), 0)
    cols = lax.broadcasted_iota(jnp.int32, (MODES * 4, count * CH), 1)
    tiled = jnp.concatenate([lift_ref[:4, :].astype(F32)] * MODES, axis=0)
    tiled = jnp.concatenate([tiled] * count, axis=1)
    mode = sum((cols >= CH * m).astype(jnp.int32) for m in range(1, count))
    return jnp.where(lax.shift_right_logical(rows, 2) == first + mode, tiled, 0.0)


def selector_last(lift_ref, count, first):
    rows = lax.broadcasted_iota(jnp.int32, (MODES, count * CH), 0)
    cols = lax.broadcasted_iota(jnp.int32, (MODES, count * CH), 1)
    tiled = jnp.concatenate([lift_ref[4:5, :].astype(F32)] * count, axis=1)
    mode = sum((cols >= CH * m).astype(jnp.int32) for m in range(1, count))
    return jnp.where(rows == first + mode, tiled, 0.0)


def mix_g_body(meta, u_ref, tx_ref, l_ref, w_ref, e_ref, r_ref, tb_ref, s_ref, p_ref, p_scr):
    u = u_ref[...].reshape(WD * 8, 128)
    s = mmh(mmh(tx_ref[...], halves(u)), selector(l_ref, 2, 2 * lax.rem(meta[3], 8)))
    s_ref[...] = s
    p_scr[...] = jnp.zeros(p_scr.shape, F32)

    def put(m, value):
        p_scr[:, CH * m : CH * (m + 1)] = value

    mix_modes(s, 2, w_ref, e_ref, r_ref, tb_ref, put)
    p_ref[...] = p_scr[...].reshape(p_ref.shape)


def mix_f_body(meta, u_ref, tx_ref, l_ref, c_ref, txc_ref, w_ref, e_ref, r_ref, tb_ref, s_ref, p_ref, v_ref, x_scr, p_scr):
    first = 8 * lax.rem(meta[3], 2)
    u = u_ref[...].reshape(WD * 8, 128)
    s = mmh(mmh(tx_ref[...], halves(u)), selector(l_ref, 8, first))
    got = c_ref[...].reshape(WD, 128)
    for p in range(PG):
        x_scr[pl.ds(p, WD, stride=PG), :] = got[:, 2 * MODES * p : 2 * MODES * (p + 1)]
    box = x_scr[pl.ds(meta[1], FX // 2), :]
    s = s + mmh(mmh(txc_ref[...], halves(box)), selector_last(l_ref, 8, first))
    s_ref[...] = s
    lift_lanes = mm(l_ref[...], e_ref[...])[4:5, :]

    def put(m, value):
        p_scr[:, CH * m : CH * (m + 1)] = value

    def extra(m, w):
        v_ref[2 * KF * m : 2 * KF * (m + 1), :] = mm((w * lift_lanes).astype(BF), r_ref[...])

    mix_modes(s, 8, w_ref, e_ref, r_ref, tb_ref, put, extra)
    p_ref[...] = p_scr[...].reshape(p_ref.shape)


K0 = math.sqrt(2.0 / math.pi)


def gelu_parts(x):
    x2 = x * x
    t = jnp.tanh(K0 * x * (1.0 + 0.044715 * x2))
    hidden = 0.5 * x * (1.0 + t)
    slope = 0.5 * (1.0 + t) + 0.5 * x * (1.0 - t * t) * (K0 * (1.0 + 3.0 * 0.044715 * x2))
    return hidden, slope


def block_pre(bb, b, zi_ref):
    rows = bb.shape[0] // 2
    lanes = slice(MODES * CL * b, MODES * CL * (b + 1))
    return mm(bb[:rows, lanes], zi_ref[: MODES * CL]) + mm(bb[rows:, lanes], zi_ref[MODES * CL :])


def lanes_of(row, b, tile_ref):
    return mmh(row[:, CL * b : CL * (b + 1)], tile_ref[...])


def point_block(point, b, tile_ref, rows):
    lanes = lanes_of(point, b, tile_ref)
    full = jnp.concatenate([lanes] * (rows // 4), axis=0)
    z_row = lax.shift_right_logical(lax.broadcasted_iota(jnp.int32, full.shape, 0), 2)
    z_col = lax.shift_right_logical(lax.broadcasted_iota(jnp.int32, full.shape, 1), 3)
    return jnp.where(z_row == z_col, full, 0.0).astype(BF)


def split(x):
    top = x.astype(BF)
    return top, (x - top.astype(F32)).astype(BF)


def mm_split(x, table):
    top, low = split(x)
    return mm(top, table) + mm(low, table)


def field_g_body(meta, x_ref, perm_ref, ty_ref, zi_ref, feat_ref, lift_ref, mix_ref, ro_ref, tile_ref, sum_ref,
                 pred_ref, slope_ref, f_scr, x_scr, acc):
    f_scr[...] = x_ref[...].astype(F32).reshape(f_scr.shape)
    for q in range(8):
        x_scr[:, 128 * q : 128 * (q + 1)] = f_scr[:, q].reshape(256, 128).astype(BF)
    bb = mm(ty_ref[meta[0]], mm(x_scr[...], perm_ref[...]).astype(BF)).astype(BF)
    point = mmh(lift_ref[...].astype(F32), mix_ref[...].astype(F32))
    readout = ro_ref[...].astype(F32)
    for b in range(NB):
        pre = block_pre(bb, b, zi_ref) + mm(feat_ref[...], point_block(point, b, tile_ref, GZ * 4))
        hidden, slope = gelu_parts(pre)
        slope_ref[b] = slope.astype(BF)
        part = hidden * lanes_of(readout, b, tile_ref)
        if b == 0:
            acc[...] = part
        else:
            acc[...] += part
    pred_ref[...] = mm_split(acc[...], sum_ref[...]).astype(BF)


def put_block(a_scr, gp, b, zf_ref):
    a = mm(gp, zf_ref[...]).astype(BF)
    rows = a.shape[0]
    width = MODES * CL
    a_scr[:rows, width * b : width * (b + 1)] = a[:, :width]
    a_scr[rows:, width * b : width * (b + 1)] = a[:, width:]


def forward_tail(a_scr, table, perm_ref):
    return mm(mm(table, a_scr[...]).astype(BF), perm_ref[...])


def field_f_body(meta, x_ref, perm_ref, ty_ref, zi_ref, feat_ref, lift_ref, mix_ref, ro_ref, tile_ref, sum_ref,
                 box_ref, zup_ref, rup_ref, cot_ref, ones_ref, zf_ref, tyf_ref, permo_ref, rdn_ref, zdn_ref,
                 pred_ref, send_ref, pt_ref, x_scr, cot_scr, a_scr, acc, acc_pt, pt_scr):
    for h in range(2):
        x_scr[:, 8 * CH * h : 8 * CH * (h + 1)] = x_ref[:, h].reshape(128, 8 * CH).astype(BF)
    bb = mm(ty_ref[...], mm(x_scr[...], perm_ref[...]).astype(BF)).astype(BF)
    for y in range(FY):
        cot_scr[PF * y : PF * (y + 1), :] = cot_ref[:, FZ * y : FZ * (y + 1)]
    wide_cot = mm_split(cot_scr[...], ones_ref[...])
    plane = box_ref[lax.div(meta[1] + meta[3], PG)]
    rows = mm(rup_ref[0], plane[:, :ZP]) + mm(rup_ref[1], plane[:, ZP:])
    cl = mm(rows.astype(BF), zup_ref[...]).astype(BF)
    point = mmh(lift_ref[...].astype(F32), mix_ref[...].astype(F32))
    readout = ro_ref[...].astype(F32)
    for b in range(NB):
        lc = jnp.concatenate([lanes_of(point[4:5], b, tile_ref)] * ZP, axis=0)
        z_row = lax.broadcasted_iota(jnp.int32, lc.shape, 0)
        z_col = lax.shift_right_logical(lax.broadcasted_iota(jnp.int32, lc.shape, 1), 3)
        lc = jnp.where(z_row == z_col, lc, 0.0).astype(BF)
        pre = block_pre(bb, b, zi_ref) + mm(feat_ref[...], point_block(point[:4], b, tile_ref, FZ * 4)) + mm(cl, lc)
        hidden, slope = gelu_parts(pre)
        ro_lanes = lanes_of(readout, b, tile_ref)
        gp = (slope * (wide_cot * ro_lanes)).astype(BF)
        part = hidden * ro_lanes
        part_pt = gp.astype(F32) * lanes_of(point[4:5], b, tile_ref)
        if b == 0:
            acc[...] = part
            acc_pt[...] = part_pt
        else:
            acc[...] += part
            acc_pt[...] += part_pt
        put_block(a_scr, gp, b, zf_ref)
    pred_ref[...] = mm_split(acc[...], sum_ref[...]).astype(BF)
    z = forward_tail(a_scr, tyf_ref[...], permo_ref)
    for h in range(2):
        send_ref[:, h] = z[:, 8 * CH * h : 8 * CH * (h + 1)].reshape(KF, 2 * PF, 8 * CH)
    pt_scr[...] = mmh(mmh(rdn_ref[...], mm_split(acc_pt[...], sum_ref[...])), zdn_ref[...])
    pt_ref[...] = pair_rows(pt_scr, 0, 1, FY // 4).astype(BF)


def dual_f_body(meta, z_ref, tx_ref, v_ref, tb_ref, pt_ref, dual_ref, q_ref, mine_ref, q_scr, o_scr):
    z = mm(tx_ref[...], z_ref[...].reshape(2 * FX, 8 * CH).astype(BF))
    rows = 2 * KF
    dual_ref[...] = z[: 2 * rows].astype(BF)
    zc, zd = z[2 * rows : 3 * rows], z[3 * rows :]
    cols = []
    for m in range(8):
        v = v_ref[rows * m : rows * (m + 1), :]
        lanes = slice(CH * m, CH * (m + 1))
        cols.append(jnp.concatenate([
            jnp.sum(v * zc[:, lanes], axis=1, keepdims=True),
            jnp.sum(v * zd[:, lanes], axis=1, keepdims=True)], axis=0))
    q_scr[...] = jnp.zeros(q_scr.shape, F32)
    q_scr[2 * GX : 2 * GX + FX, :] = mmh(tb_ref[...], jnp.concatenate(cols, axis=1))
    o_scr[: 2 * GX, :] = q_scr[pl.ds(2 * GX - 2 * meta[1], 2 * GX), :]
    lanes = [o_scr[pl.ds(r, WD, stride=8), :] for r in range(8)]
    lanes.append(jnp.zeros((WD, 64), F32))
    q_ref[...] = jnp.concatenate(lanes, axis=1).reshape(q_ref.shape)
    for p in range(PG):
        at = PG * meta[3] + p - meta[1]
        ok = jnp.logical_and(at >= 0, at < WD)
        plane = pt_ref[jnp.clip(at, 0, WD - 1)]
        mine_ref[32 * p : 32 * (p + 1), :] = jnp.where(ok, plane, jnp.zeros_like(plane))


def grad_modes(modes, s_ref, d_ref, e_ref, o_ref, g_ref):
    rows = 2 * KF
    for m in range(modes):
        lanes = slice(CH * m, CH * (m + 1))
        sa = mm(s_ref[:rows, lanes].astype(BF), e_ref[...])
        sb = mm(s_ref[rows:, lanes].astype(BF), e_ref[...])
        za = mm(d_ref[:rows, lanes], o_ref[...])
        zb = mm(d_ref[rows:, lanes], o_ref[...])
        g_ref[m] = (sa * za + sb * zb).reshape(KF, 2, CC)


def grad_f_body(s_ref, d_ref, e_ref, o_ref, g_ref):
    grad_modes(8, s_ref, d_ref, e_ref, o_ref, g_ref)


def dual_g_body(z_ref, tx_ref, s_ref, e_ref, o_ref, g_ref, d_scr):
    z = z_ref[...].reshape(2 * GX, 128)[:, : 2 * CH]
    d_scr[...] = mm(tx_ref[...], z.astype(BF)).astype(BF)
    grad_modes(2, s_ref, d_scr, e_ref, o_ref, g_ref)


def back_g_body(meta, q_ref, dd_ref, ty_ref, pt_ref, cot_ref, slope_ref, ro_ref, tile_ref, ones_ref, zf_ref, tyf_ref,
                permo_ref, send_ref, cot_scr, pad_scr, a_scr):
    level = meta[0]
    cot_scr[...] = jnp.zeros(cot_scr.shape, F32)
    for y in range(YG):
        cot_scr[PG * y : PG * (y + 1), :GZ] = cot_ref[:, GZ * y : GZ * (y + 1)]
    q = q_ref[...].reshape(LV * WD, 128)[:, :64]
    odd = jnp.bitwise_and(lax.broadcasted_iota(jnp.int32, q.shape, 0), 1) == 1
    q = jnp.concatenate([jnp.where(odd, 0.0, q), jnp.where(odd, q, 0.0)], axis=1).astype(BF)
    g = mm(q, dd_ref[...]).astype(BF)
    total = jnp.zeros((YG, PG * ZP), F32)
    for l in range(LV):
        start = pl.multiple_of(192 + YG * level - meta[4 + l], 8)
        for k in range(4):
            t = ty_ref[k, pl.ds(start, YG), :].astype(BF)
            total += mm(t, g[WD * l : WD * (l + 1), PG * ZP * k : PG * ZP * (k + 1)])
    for p in range(PG):
        cot_scr[pl.ds(p, YG, stride=PG), :] += total[:, ZP * p : ZP * (p + 1)]
    pad_scr[...] = jnp.zeros(pad_scr.shape, F32)
    planes = [jnp.zeros((32, 128), F32) for _ in range(PG)]
    for l in range(LV):
        start = 96 + 32 * level - lax.div(meta[4 + l], 2)
        for p in range(PG):
            pad_scr[l, p, 96:128, :] = pt_ref[l, 32 * p : 32 * (p + 1), :].astype(F32)
            planes[p] += pad_scr[l, p, pl.ds(start, 32), :]
    for p in range(PG):
        for k in range(2):
            cot_scr[pl.ds(PG * k + p, 32, stride=2 * PG), :] += planes[p][:, ZP * k : ZP * (k + 1)]
    wide_cot = mm_split(cot_scr[...], ones_ref[...])
    readout = ro_ref[...].astype(F32)
    for b in range(NB):
        gp = (slope_ref[b].astype(F32) * (wide_cot * lanes_of(readout, b, tile_ref))).astype(BF)
        put_block(a_scr, gp, b, zf_ref)
    send_ref[...] = forward_tail(a_scr, tyf_ref[level], permo_ref).astype(BF).reshape(send_ref.shape)


def here():
    return lax.axis_index("level"), lax.axis_index("wide")


def greet(with_level, with_wide):
    level, wide = here()
    barrier = pltpu.get_barrier_semaphore()
    count = 0
    if with_level:
        for i in range(1, LV):
            pl.semaphore_signal(barrier, inc=1, device_id=(lax.rem(level + i, LV), wide), device_id_type=MESH)
        count += LV - 1
    if with_wide:
        def one(i, carry):
            pl.semaphore_signal(barrier, inc=1, device_id=(level, lax.rem(wide + i, WD)), device_id_type=MESH)
            return carry

        lax.fori_loop(1, WD, one, 0)
        count += WD - 1
    return barrier, count


def remote(src, dst, sems, to):
    return pltpu.make_async_remote_copy(
        src_ref=src, dst_ref=dst, send_sem=sems.at[0], recv_sem=sems.at[1], device_id=to, device_id_type=MESH)


def push_wide(pairs):
    level, wide = here()

    def one(i, carry):
        peer = lax.rem(wide + i, WD)
        for source, land, sems in pairs:
            remote(source(peer), land.at[wide], sems, (level, peer)).start()
        return carry

    lax.fori_loop(1, WD, one, 0)


def push_level(source, land, sems):
    level, wide = here()
    for i in range(1, LV):
        peer = lax.rem(level + i, LV)
        remote(source(peer), land.at[level], sems, (peer, wide)).start()


def finish(land, sems, count):
    level, wide = here()
    part = land.at[pl.ds(0, count - 1)]
    done = remote(part, part, sems, (level, wide))
    done.wait_send()
    done.wait_recv()


def exchange_in_body(kg_ref, kf_ref, out_ref, land, msg, s_level, s_wide):
    level, wide = here()
    barrier, count = greet(True, True)
    msg[...] = jnp.zeros(msg.shape, F32)
    for w in range(WD):
        msg[w, PG : PG + PF, :] = kf_ref[w // 2]
    land[level] = kg_ref[pl.ds(8 * level, 8)]
    pl.semaphore_wait(barrier, count)
    push_level(lambda peer: kg_ref.at[pl.ds(8 * peer, 8)], land, s_level)
    finish(land, s_level, LV)
    total = land[0] + land[1] + land[2] + land[3]
    for w in range(WD):
        msg[w, :PG, :] = total[w // 8]
    push_wide([(lambda peer: msg.at[peer], out_ref, s_wide)])
    out_ref[wide] = msg[wide]
    finish(out_ref, s_wide, WD)


def exchange_g_body(p_ref, out_ref, land, s_wide, s_level):
    level, wide = here()
    barrier, count = greet(True, True)
    land[wide] = p_ref[wide]
    pl.semaphore_wait(barrier, count)
    push_wide([(lambda peer: p_ref.at[peer], land, s_wide)])
    finish(land, s_wide, WD)
    out_ref[level] = land[...].reshape(WD * 8, 128).astype(BF)
    push_level(lambda peer: out_ref.at[level], out_ref, s_level)
    finish(out_ref, s_level, LV)


def gather_level_body(x_ref, out_ref, s_level):
    level, wide = here()
    barrier, count = greet(True, False)
    out_ref[level] = x_ref[...]
    pl.semaphore_wait(barrier, count)
    push_level(lambda peer: x_ref, out_ref, s_level)
    finish(out_ref, s_level, LV)


def exchange_box_body(spec_ref, planes_ref, got_ref, box_ref, s_spec, s_box):
    level, wide = here()
    barrier, count = greet(False, True)
    got_ref[wide] = spec_ref[wide // 2]
    box_ref[wide] = planes_ref[wide % PG]
    pl.semaphore_wait(barrier, count)
    push_wide([(lambda peer: spec_ref.at[peer // 2], got_ref, s_spec),
               (lambda peer: planes_ref.at[peer % PG], box_ref, s_box)])
    finish(got_ref, s_spec, WD)
    finish(box_ref, s_box, WD)


def exchange_f_body(x_ref, out_ref, s_wide):
    level, wide = here()
    barrier, count = greet(False, True)
    out_ref[wide] = x_ref[wide]
    pl.semaphore_wait(barrier, count)
    push_wide([(lambda peer: x_ref.at[peer], out_ref, s_wide)])
    finish(out_ref, s_wide, WD)


def exchange_dual_body(x_ref, pt_ref, out_ref, all_ref, s_wide, s_pt):
    level, wide = here()
    barrier, count = greet(False, True)
    out_ref[wide] = x_ref[wide]
    all_ref[wide] = pt_ref[...]
    pl.semaphore_wait(barrier, count)
    push_wide([(lambda peer: x_ref.at[peer], out_ref, s_wide), (lambda peer: pt_ref, all_ref, s_pt)])
    finish(out_ref, s_wide, WD)
    finish(all_ref, s_pt, WD)


def exchange_back_body(q_ref, pt_ref, out_ref, pts_ref, s_wide, s_level, s_pt):
    level, wide = here()
    barrier, count = greet(True, True)
    own = out_ref.at[level]
    own[wide] = q_ref[wide]
    pts_ref[level] = pt_ref[...]
    pl.semaphore_wait(barrier, count)
    push_level(lambda peer: pt_ref, pts_ref, s_pt)
    push_wide([(lambda peer: q_ref.at[peer], own, s_wide)])
    finish(own, s_wide, WD)
    push_level(lambda peer: out_ref.at[level], out_ref, s_level)
    finish(out_ref, s_level, LV)
    finish(pts_ref, s_pt, LV)


def exchange_out_body(x_ref, out_ref, land, msg, s_level, s_wide):
    level, wide = here()
    barrier, count = greet(True, True)
    msg[...] = jnp.zeros(msg.shape, F32)
    land[level] = x_ref[level]
    pl.semaphore_wait(barrier, count)
    push_level(lambda peer: x_ref.at[peer], land, s_level)
    finish(land, s_level, LV)
    total = land[0].astype(F32) + land[1].astype(F32) + land[2].astype(F32) + land[3].astype(F32)
    for q in range(8):
        msg[:, q, :, : 2 * CH] = total[:, 2 * CH * q : 2 * CH * (q + 1)].reshape(8, 8, 2 * CH)
    push_wide([(lambda peer: msg.at[peer // 8, peer % 8], out_ref, s_wide)])
    out_ref[wide] = msg[wide // 8, wide % 8]
    finish(out_ref, s_wide, WD)


def shards(coarse_input, fine_input, coarse_cotangent, fine_cotangent, well_x, well_y, coarse_lift, coarse_mixing,
           coarse_spectral, coarse_readout, fine_lift, fine_mixing, fine_spectral, fine_readout):
    level = lax.axis_index("level")
    wide = lax.axis_index("wide")
    meta = jnp.concatenate([
        jnp.stack([level, well_x[level], 8 * well_y[level], wide]).astype(jnp.int32), 8 * well_y])
    row_g, row_f = coarse_readout[None], fine_readout
    lift_f, mixing_f = fine_lift[0], fine_mixing[0]

    feat_g, kg = run(features_g_body, [((256, GZ * 4), BF), ((KF, PG, 128), F32)],
                     coarse_input, Z4_G, TYA_G, meta=meta, scratch=[vm((256, GZ * 4))], name="features_g")
    feat_f, kf = run(features_f_body, [((256, FZ * 4), BF), ((KF, PF, 128), F32)],
                     fine_input[0], Z4_F, TYA_F, scratch=[vm((256, FZ * 4))], name="features_f")
    (got_in,) = run(exchange_in_body, [((WD, 8, 128), F32)], kg, kf,
                    scratch=[vm((LV, 8, PG, 128)), vm((WD, 8, 128)), DMA2, DMA2], cid=1, name="exchange_in")
    s_g, p_g = run(mix_g_body, [((4 * KF, 2 * CH), F32), ((WD, 8, 128), F32)],
                   got_in, TXS_G, coarse_lift, coarse_spectral, SPREAD_IN, FOLD_IN, TXB_G, meta=meta,
                   scratch=[vm((2 * GX, 128))], name="mix_g")
    (x_g,) = run(exchange_g_body, [((LV, WD * 8, 128), BF)], p_g,
                 scratch=[vm((WD, 8, 128)), DMA2, DMA2], cid=2, name="exchange_g")
    pred_g, slope_g = run(
        field_g_body, [((256, ZP), BF), ((NB, 256, ZP * CL), BF)],
        x_g, PERM_WIDE, TYI_G, ZI_G, feat_g, coarse_lift, coarse_mixing, row_g, TILE_CL, SUM_CL, meta=meta,
        scratch=[vm((KF, 8, 8, 128)), vm((256, 1024), BF), vm((256, ZP * CL))], name="field_g")
    (rows_all,) = run(gather_level_body, [((LV, 256, ZP), BF)], pred_g, scratch=[DMA2], cid=3, name="gather_rows")
    spec_c, planes_c = run(
        box_body, [((KF, 1, 128), F32), ((PG, 32, 128), BF)], rows_all, ZC, TYA_BOX, meta=meta,
        scratch=[vm((LV * 256, ZP)), vm((256, ZP)), vm((2 * KF * PG, MODES)), vm((KF, 128))], name="box")
    got_c, box_c = run(exchange_box_body, [((WD, 1, 128), F32), ((WD, 32, 128), BF)], spec_c, planes_c,
                       scratch=[DMA2, DMA2], cid=4, name="exchange_box")
    s_f, p_f, v_f = run(
        mix_f_body, [((4 * KF, 8 * CH), F32), ((WD, 2 * PF, 8 * CH), F32), ((8 * 2 * KF, CH), F32)],
        got_in, TXS_F, lift_f, got_c, TXS_BOX, fine_spectral[0], SPREAD_IN, FOLD_IN, TXB_F, meta=meta,
        scratch=[vm((GX, 2 * MODES)), vm((2 * FX, 8 * CH))], name="mix_f")
    (x_f,) = run(exchange_f_body, [((WD, 2 * PF, 8 * CH), F32)], p_f, scratch=[DMA2], cid=5, name="exchange_f")
    pred_f, send_f, pt_f = run(
        field_f_body, [((256, FZ), BF), ((KF, 2, 2 * PF, 8 * CH), F32), ((32, 128), BF)],
        x_f.reshape(KF, 2, 2 * PF, 8 * CH), PERM_IN, TYI_F, ZI_F, feat_f, lift_f, mixing_f, row_f, TILE_CL, SUM_CL,
        box_c, Z_UP, ROWS_UP, fine_cotangent[0], ONES_CL, ZF_F, TYF_F, PERM_OUT, ROWS_DOWN, Z_DOWN, meta=meta,
        scratch=[vm((128, MODES * CH), BF), vm((256, FZ)), vm((512, MODES * CH), BF), vm((256, ZP * CL)),
                 vm((256, ZP * CL)), vm((FY // 2, ZP))], name="field_f")
    got_f, pts = run(exchange_dual_body, [((WD, 2 * PF, 8 * CH), F32), ((WD, 32, 128), BF)],
                     send_f.reshape(WD, 2 * PF, 8 * CH), pt_f, scratch=[DMA2, DMA2], cid=6, name="exchange_dual")
    dual_f, q_f, mine = run(
        dual_f_body, [((4 * KF, 8 * CH), BF), ((WD, 1, 128), F32), ((128, 128), BF)],
        got_f, TXD_F, v_f, TXB_BOX, pts, meta=meta,
        scratch=[vm((2 * GX + 2 * GX, 8)), vm((2 * GX, 8))], name="dual_f")
    q_all, pt_all = run(exchange_back_body, [((LV, WD, 1, 128), F32), ((LV, 128, 128), BF)], q_f, mine,
                        scratch=[DMA2, DMA2, DMA2], cid=7, name="exchange_back")
    (send_g,) = run(
        back_g_body, [((LV, 64, MODES * CH), BF)],
        q_all, DD_BOX, TYB_BOX, pt_all, coarse_cotangent, slope_g, row_g, TILE_CL, ONES_CL, ZF_G, TYF_G, PERM_OUT,
        meta=meta, scratch=[vm((256, ZP)), vm((LV, PG, 224, 128)), vm((512, MODES * CH), BF)], name="back_g")
    (got_g,) = run(exchange_out_body, [((WD, 8, 128), F32)], send_g,
                   scratch=[vm((LV, 64, MODES * CH), BF), vm((8, 8, 8, 128)), DMA2, DMA2], cid=8, name="exchange_out")
    (grad_g,) = run(dual_g_body, [((2, KF, 2, CC), F32)], got_g, TXD_G, s_g, SPREAD_IN, SPREAD_OUT,
                    scratch=[vm((4 * KF, 2 * CH), BF)], name="dual_g")
    (grad_f,) = run(grad_f_body, [((8, KF, 2, CC), F32)], s_f, dual_f, SPREAD_IN, SPREAD_OUT, name="grad_f")
    coarse_out = pred_g.reshape(YG, PG, ZP).transpose(1, 0, 2)[:, :, :GZ].reshape(PG, YG * GZ)
    fine_out = pred_f.reshape(FY, PF, FZ).transpose(1, 0, 2).reshape(1, PF, FY * FZ)
    return coarse_out, fine_out, grad_g, grad_f[None]


def solution(mesh):
    placed = (
        P("wide", "level"),
        P("level", "wide", None),
        P("wide", "level"),
        P("level", "wide", None),
        P(),
        P(),
        P(),
        P(),
        P(("level", "wide"), None, None, None),
        P(),
        P("level", None, None),
        P("level", None, None),
        P("level", "wide", None, None, None),
        P("level", None),
    )
    return jax.shard_map(
        shards,
        mesh=mesh,
        in_specs=placed,
        out_specs=(
            P("wide", "level"),
            P("level", "wide", None),
            P(("level", "wide"), None, None, None),
            P("level", "wide", None, None, None),
        ),
        check_vma=False,
    )
```

```python
import math

import ml_dtypes
import numpy as np
import jax
import jax.numpy as jnp
from jax import lax
from jax.experimental import pallas as pl
from jax.experimental.pallas import tpu as pltpu
from jax.sharding import PartitionSpec as P

MODES = 16
KF = 2 * MODES
CH = 48
NB = 6
CL = 8
GX = 256
GY = 256
GZ = 50
FX = 128
FY = 128
FZ = 64
ZP = 64
LV = 4
WD = 64
PG = 4
YG = 64
PF = 2
CC = CH * CH
BF = jnp.bfloat16
F32 = jnp.float32
HIGH = lax.Precision.HIGHEST
VMEM_BYTES = 60 * 2**20


def bf(x):
    return np.asarray(x, np.float32).astype(ml_dtypes.bfloat16)


def f32(x):
    return np.asarray(x, np.float32)


def waves(rows, length):
    j = np.arange(KF)
    signed = np.where(j < MODES, j, j - KF)
    turn = np.mod(rows[:, None] * signed[None, :], length) * (2.0 * math.pi / length)
    return np.cos(turn) / math.sqrt(length), np.sin(turn) / math.sqrt(length)


def forward_table(rows, length):
    c, s = waves(rows, length)
    c, s = c.T, s.T
    return np.stack([np.stack([c, s], 1), np.stack([-s, c], 1)], 0)


def depth(length):
    c, s = waves(np.arange(length), length)
    both = np.stack([c[:, :MODES], -s[:, :MODES]], 1)
    both = bf(both).astype(np.float64)
    return np.concatenate([both, np.zeros((ZP - length, 2, MODES))], 0)


D_G, D_F = depth(GZ), depth(FZ)
ZMAP = np.zeros((ZP, FZ))
ZMAP[np.arange(FZ) * GZ // FZ, np.arange(FZ)] = 1.0
D_POOL = np.einsum("gf,frk->grk", ZMAP, D_F)


def depth_blocks(d):
    return np.einsum("zrk,ij->zirkj", d, np.eye(CL)).reshape(ZP * CL, 2 * MODES * CL)


def depth_features(d, length):
    return np.einsum("zrk,ij->zirkj", d[:length], np.eye(4)).reshape(length * 4, 2 * MODES * 4)


ZF_G, ZF_F = bf(depth_blocks(D_G)), bf(depth_blocks(D_F))
ZI_G, ZI_F = bf(depth_blocks(D_G).T), bf(depth_blocks(D_F).T)
Z4_G, Z4_F = bf(depth_features(D_G, GZ)), bf(depth_features(D_F, FZ))
ZC = f32(D_POOL.reshape(ZP, 2 * MODES))

FY_G = np.stack([forward_table(v * YG + np.arange(YG), GY) for v in range(LV)], 0)
FY_F = forward_table(np.arange(FY), FY)
FY_BOX = FY_F.reshape(2, KF, 2, FY // 2, 2).sum(4)
FX_G = forward_table(np.arange(GX), GX)
FX_F = forward_table(np.arange(FX), FX)
FX_BOX = FX_F.reshape(2, KF, 2, FX // 2, 2).sum(4)
EYE_G, EYE_F = np.eye(PG), np.eye(PF)

TYA_G = f32(np.einsum("vakbt,pq->vakpbtq", FY_G, EYE_G).reshape(LV, 2 * KF * PG, 2 * YG * PG))
TYA_F = f32(np.einsum("akbt,pq->akpbtq", FY_F, EYE_F).reshape(2 * KF * PF, 2 * FY * PF))
TYA_BOX = f32(np.einsum("akbt,pq->akpbtq", FY_BOX, EYE_G).reshape(2 * KF * PG, FY * PG))
TYF_G = bf(np.einsum("vakbt,pq->vkpabtq", FY_G, EYE_G).reshape(LV, KF * PG * 2, 2 * YG * PG))
TYF_F = bf(np.einsum("akbt,pq->kpabtq", FY_F, EYE_F).reshape(KF * PF * 2, 2 * FY * PF))
TYI_G = bf(np.einsum("vbkat,pq->vatpkqb", FY_G, EYE_G).reshape(LV, 2 * YG * PG, KF * PG * 2))
TYI_F = bf(np.einsum("bkat,pq->atpkqb", FY_F, EYE_F).reshape(2 * FY * PF, KF * PF * 2))
TYB_BOX = bf(np.repeat(FY_BOX.transpose(3, 2, 0, 1).reshape(FY // 2, 4 * KF), 2, axis=1))
DD_BOX = bf(np.einsum("zahk,pq,rs->hprkasqz", D_POOL.reshape(ZP, 2, 2, 8), EYE_G, np.eye(2)).reshape(128, 4 * PG * ZP))


def source_rows(table):
    a = np.stack([table[0], -table[1]], 1)
    b = np.stack([table[1], table[0]], 1)
    return np.stack([a, b], 0).reshape(4 * KF, 2, -1)


def in_rows(table, planes, first):
    rows = source_rows(table).reshape(4 * KF, 2, WD, planes)
    out = np.zeros((4 * KF, 2, WD, 8))
    out[..., first : first + planes] = rows
    return out.reshape(4 * KF, 2 * WD * 8)


TXS_G = f32(in_rows(FX_G, PG, 0))
TXS_F = f32(in_rows(FX_F, PF, PG))
TXS_BOX = f32(source_rows(FX_BOX).reshape(4 * KF, FX))


def dual_rows(table, count):
    r, i = table[0], table[1]
    kinds = [np.stack([r, r], 1), np.stack([i, i], 1), np.stack([r, i], 1), np.stack([i, -r], 1)]
    rows = np.stack(kinds[:count], 0).transpose(0, 1, 2, 4, 3)
    return rows.reshape(count * 2 * KF, -1)


TXD_G = bf(dual_rows(FX_G, 2))
TXD_F = bf(dual_rows(FX_F, 4))


def back_rows(table):
    back = table.transpose(3, 2, 0, 1)
    back = np.stack([back, back], 4)
    return back.reshape(back.shape[0] * 2, 4 * KF)


TXB_G = bf(back_rows(FX_G))
TXB_F = bf(back_rows(FX_F))
TXB_BOX = f32(back_rows(FX_BOX))

PERM = np.zeros((MODES, NB, CL, NB, MODES, CL))
for _k in range(MODES):
    for _b in range(NB):
        for _l in range(CL):
            PERM[_k, _b, _l, _b, _k, _l] = 1.0
PERM = PERM.reshape(MODES * CH, MODES * CH)
PERM_OUT = bf(PERM.T)
PERM_WIDE = np.zeros((8, 128, MODES * CH))
PERM_WIDE[:, : 2 * CH] = PERM.reshape(8, 2 * CH, MODES * CH)
PERM_WIDE = PERM_WIDE.reshape(1024, MODES * CH)
PERM_WIDE, PERM_WIDE_OUT = bf(PERM_WIDE), bf(PERM_WIDE.T)
SPREAD_IN = bf(np.kron(np.eye(CH), np.ones((1, CH))))
CHUNK = 8 * CH
TILE_OUT = bf(np.kron(np.ones((1, 8)), np.eye(CH)))
FOLD = bf(np.kron(np.ones((8, 1)), np.eye(CH)))
ONES_CL = bf(np.kron(np.eye(ZP), np.ones((1, CL))))
SUM_CL = bf(np.kron(np.eye(ZP), np.ones((CL, 1))))
TILE_CL = f32(np.kron(np.ones((1, ZP)), np.eye(CL)))
ROWS_UP = np.kron(np.eye(FY // 2), np.ones((2 * PF, 1))).reshape(256, FY // 4, 2).transpose(2, 0, 1)
ROWS_UP = bf(ROWS_UP)
ROWS_DOWN = f32(np.kron(np.eye(FY // 2), np.ones((1, 2 * PF))))
Z_UP = bf(ZMAP)
Z_DOWN = f32(ZMAP.T)


def mm(a, b):
    return jnp.dot(a, b, preferred_element_type=F32)


def mmh(a, b):
    return jnp.dot(a, b, preferred_element_type=F32, precision=HIGH)


MESH = pl.DeviceIdType.MESH
DMA2 = pltpu.SemaphoreType.DMA((2,))


def vm(shape, kind=F32):
    return pltpu.VMEM(shape, kind)


BY_LEVEL = ("tya_g", "tyi_g", "tyf_g")


def run(body, outs, smem, inputs, scratch, sems=(), kept=(), cid=None, name=None):
    held = {n: vm(t.shape[1:] if n in BY_LEVEL else t.shape, t.dtype) for n, t in inputs.items()}

    def kernel(*refs):
        refs = list(refs)

        def take(names):
            got = {n: refs.pop(0) for n in names}
            return got

        scalars = take(smem)
        given = take(inputs)
        res = take(outs)
        scr = take(scratch)
        sem = take(sems)
        inside = take(held)
        load_sem = refs.pop(0)
        level = lax.axis_index("level")
        copies, started, ready = {}, set(), set()
        for k, n in enumerate(inputs):
            src = given[n].at[level] if n in BY_LEVEL else given[n]
            copies[n] = pltpu.make_async_copy(src, inside[n], load_sem.at[k])

        def start(names):
            for n in names:
                if n not in started:
                    copies[n].start()
                    started.add(n)

        def get(n):
            if n not in ready:
                copies[n].wait()
                ready.add(n)
            return inside[n]

        body(scalars, start, get, res, scr, sem)

    got = pl.pallas_call(
        kernel,
        out_shape=[jax.ShapeDtypeStruct(s, d) for s, d in outs.values()],
        in_specs=[pl.BlockSpec(memory_space=pltpu.SMEM)] * len(smem) + [pl.BlockSpec(memory_space=pl.ANY)] * len(inputs),
        out_specs=[pl.BlockSpec(memory_space=pl.ANY if n in kept else pltpu.VMEM) for n in outs],
        scratch_shapes=[vm(*v) for v in scratch.values()] + [DMA2] * len(sems) + list(held.values())
        + [pltpu.SemaphoreType.DMA((len(held),))],
        name=name,
        compiler_params=pltpu.CompilerParams(
            vmem_limit_bytes=VMEM_BYTES, collective_id=cid, has_side_effects=cid is not None),
    )(*smem.values(), *inputs.values())
    return dict(zip(outs, got))


def halves(u):
    half = u.shape[1] // 2
    return jnp.concatenate([u[:, :half], u[:, half:]], axis=0)


def features(rows, planes, width, x_ref, z, table, feat_ref, out_ref, scr):
    for y in range(rows):
        scr[planes * y : planes * (y + 1), :] = x_ref[:, width * y : width * (y + 1)].astype(F32)
    feat = scr[...].astype(BF)
    feat_ref[...] = feat
    both = mmh(table, halves(mm(feat, z)))
    rows_out = both.shape[0] // 2
    lanes = jnp.concatenate([both[:rows_out], both[rows_out:]], axis=1)
    out_ref[...] = lanes.reshape(out_ref.shape)


def stack_modes(x, modes, lane):
    return jnp.concatenate([x[:, lane(m) : lane(m) + CH] for m in range(modes)], axis=0).astype(BF)


def lane_g(m):
    return CH * m


def lane_f(m):
    return 128 * (m // 2) + CH * (m % 2)


def weights_chunk(w_ref, c):
    w = w_ref[:, :, :, CHUNK * c : CHUNK * (c + 1)].astype(F32)
    return w.reshape(w.shape[0] * 2 * KF, CHUNK)


def mix_modes(s, modes, w_ref, spread, fold, table, acc_a, acc_b):
    half = 2 * KF
    sa, sb = stack_modes(s[:half], modes, lane_g), stack_modes(s[half:], modes, lane_g)
    for c in range(CC // CHUNK):
        w = weights_chunk(w_ref, c)
        e = spread[:, CHUNK * c : CHUNK * (c + 1)]
        if c == 0:
            acc_a[...] = w * mm(sa, e)
            acc_b[...] = w * mm(sb, e)
        else:
            acc_a[...] += w * mm(sa, e)
            acc_b[...] += w * mm(sb, e)
    pa, pb = mm(acc_a[...].astype(BF), fold).astype(BF), mm(acc_b[...].astype(BF), fold).astype(BF)
    spare = jnp.zeros((2 * half, 128 - 2 * CH), BF)
    parts = []
    for m in range(modes):
        parts.append(jnp.concatenate([pa[half * m : half * (m + 1)], pb[half * m : half * (m + 1)]], axis=0))
        if m % 2 == 1:
            parts.append(spare)
    return mm(table, jnp.concatenate(parts, axis=1))


def grad_modes(sa, sb, za, zb, spread, put):
    for c in range(CC // CHUNK):
        e = spread[:, CHUNK * c : CHUNK * (c + 1)]
        g = mm(sa, e) * za + mm(sb, e) * zb
        put(slice(CHUNK * c, CHUNK * (c + 1)), g.reshape(g.shape[0] // (2 * KF), KF, 2, CHUNK))


def shift_rows(rows, cols, by, group_rows=None):
    r = lax.broadcasted_iota(jnp.int32, (rows, cols), 0)
    c = lax.broadcasted_iota(jnp.int32, (rows, cols), 1)
    hit = c - r == by
    if group_rows is not None:
        shift = group_rows.bit_length() - 1
        hit = jnp.logical_and(hit, lax.shift_right_logical(r, shift) == lax.shift_right_logical(c, shift))
    return jnp.where(hit, 1.0, 0.0)


def pick_plane(planes, at):
    which = lax.broadcasted_iota(jnp.int32, planes.shape, 0)
    return jnp.sum(jnp.where(which == at, planes, 0.0), axis=0)


def pair_rows(scr, first, stride, count):
    even = scr[pl.ds(first, count, stride=2 * stride), :]
    odd = scr[pl.ds(first + stride, count, stride=2 * stride), :]
    return jnp.concatenate([even, odd], axis=1)


def selector(lift, count, first, features_in):
    shape = (MODES * features_in, count * CH)
    rows = lax.broadcasted_iota(jnp.int32, shape, 0)
    cols = lax.broadcasted_iota(jnp.int32, shape, 1)
    tiled = jnp.concatenate([lift] * MODES, axis=0) if features_in > 1 else lift
    tiled = jnp.concatenate([tiled] * count, axis=1)
    mode = sum((cols >= CH * m).astype(jnp.int32) for m in range(1, count))
    kz = lax.shift_right_logical(rows, 2) if features_in > 1 else rows
    return jnp.where(kz == first + mode, tiled, 0.0)


K0 = math.sqrt(2.0 / math.pi)


def gelu_parts(x):
    x2 = x * x
    t = jnp.tanh(K0 * x * (1.0 + 0.044715 * x2))
    hidden = 0.5 * x * (1.0 + t)
    slope = 0.5 * (1.0 + t) + 0.5 * x * (1.0 - t * t) * (K0 * (1.0 + 3.0 * 0.044715 * x2))
    return hidden, slope


def block_pre(bb, b, zi):
    rows = bb.shape[0] // 2
    lanes = slice(MODES * CL * b, MODES * CL * (b + 1))
    return mm(bb[:rows, lanes], zi[: MODES * CL]) + mm(bb[rows:, lanes], zi[MODES * CL :])


def lanes_of(row, b, tile):
    return mmh(row[:, CL * b : CL * (b + 1)], tile)


def point_block(point, b, tile, shift):
    count = point.shape[0]
    full = jnp.concatenate([lanes_of(point, b, tile)] * ZP, axis=0)
    z_row = lax.shift_right_logical(lax.broadcasted_iota(jnp.int32, full.shape, 0), shift)
    z_col = lax.shift_right_logical(lax.broadcasted_iota(jnp.int32, full.shape, 1), 3)
    return jnp.where(z_row == z_col, full, 0.0).astype(BF)


def split(x):
    top = x.astype(BF)
    return top, (x - top.astype(F32)).astype(BF)


def mm_split(x, table):
    top, low = split(x)
    return mm(top, table) + mm(low, table)


def put_block(a_scr, gp, b, zf):
    a = mm(gp, zf).astype(BF)
    rows = a.shape[0]
    width = MODES * CL
    a_scr[:rows, width * b : width * (b + 1)] = a[:, :width]
    a_scr[rows:, width * b : width * (b + 1)] = a[:, width:]


def forward_tail(a_scr, table, perm):
    return mm(mm(table, a_scr[...]).astype(BF), perm)


def here():
    return lax.axis_index("level"), lax.axis_index("wide")


def greet():
    level, wide = here()
    barrier = pltpu.get_barrier_semaphore()
    for i in range(1, LV):
        pl.semaphore_signal(barrier, inc=1, device_id=(lax.rem(level + i, LV), wide), device_id_type=MESH)

    def one(i, carry):
        pl.semaphore_signal(barrier, inc=1, device_id=(level, lax.rem(wide + i, WD)), device_id_type=MESH)
        return carry

    lax.fori_loop(1, WD, one, 0)
    return barrier, LV - 1 + WD - 1


def remote(src, dst, sems, to):
    return pltpu.make_async_remote_copy(
        src_ref=src, dst_ref=dst, send_sem=sems.at[0], recv_sem=sems.at[1], device_id=to, device_id_type=MESH)


def push_wide(source, land, sems):
    level, wide = here()

    def one(i, carry):
        peer = lax.rem(wide + i, WD)
        remote(source(peer), land.at[wide], sems, (level, peer)).start()
        return carry

    lax.fori_loop(1, WD, one, 0)


def push_level(source, land, sems):
    level, wide = here()
    for i in range(1, LV):
        peer = lax.rem(level + i, LV)
        remote(source(peer), land.at[level], sems, (peer, wide)).start()


def finish(land, sems, count):
    level, wide = here()
    part = land.at[pl.ds(0, count - 1)]
    done = remote(part, part, sems, (level, wide))
    done.wait_send()
    done.wait_recv()


SEMS = ("in_level", "in", "g", "g_level", "rows", "spec", "box", "f", "dual", "pts", "q", "q_level", "pt_level",
        "out_level", "got_g")
RESULTS = {
    "pred_g": ((256, ZP), F32), "pred_f": ((256, FZ), F32), "s_g": ((4 * KF, 2 * CH), F32),
    "s_f": ((4 * KF, 8 * CH), F32), "dual_f": ((4 * KF, 512), BF), "got_g": ((WD, 8, 128), F32),
}
LANDS = {
    "in_level": ((LV, 8, PG, 128), F32), "in": ((WD, 8, 128), F32), "g": ((WD, 8, 128), F32),
    "g_level": ((LV, WD * 8, 128), BF), "rows": ((LV, 256, ZP), BF), "spec": ((WD, 1, 128), F32),
    "box": ((WD, 32, 128), BF), "f": ((WD, 16, 128), BF), "dual": ((WD, 16, 128), BF), "pts": ((WD, 32, 128), BF),
    "q": ((LV, WD, 1, 128), F32), "pt_level": ((LV, 128, 128), BF), "out_level": ((LV, 64, MODES * CH), BF),
}
SCRATCH = {
    "x_g": ((256, GZ * 4), F32), "x_ff": ((256, FZ * 4), F32), "feat_g": ((256, GZ * 4), BF), "feat_f": ((256, FZ * 4), BF),
    "kg": ((KF, PG, 128), F32), "kf": ((KF, PF, 128), F32), "cot_f": ((256, FZ), F32),
    "msg_in": ((WD, 8, 128), F32), "p_gm": ((WD, 8, 128), F32), "mix_a": ((512, CHUNK), F32), "mix_b": ((512, CHUNK), F32),
    "mix_ga": ((128, CHUNK), F32), "mix_gb": ((128, CHUNK), F32), "wide_cot": ((256, ZP * CL), F32),
    "x_wide": ((KF, 8, 8, 128), F32), "x_in": ((256, 1024), BF), "acc": ((256, ZP * CL), F32),
    "acc_pt": ((256, ZP * CL), F32), "slope": ((NB, 256, ZP * CL), BF), "pred_b": ((256, ZP), BF),
    "box_f": ((256, ZP), F32), "s_box": ((2 * KF * PG, MODES), F32),
    "o_box": ((KF, 128), F32), "spec_m": ((KF, 1, 128), F32), "planes_m": ((PG, 32, 128), BF),
    "x_box": ((GX, 2 * MODES), F32), "p_f": ((4 * 2 * FX, 128), F32), "p_fm": ((WD, 16, 128), BF),
    "v_f": ((8 * 2 * KF, CH), F32), "lm_g": ((NB, GZ * 4, ZP * CL), BF), "lm_f": ((NB, FZ * 4, ZP * CL), BF),
    "lc_f": ((NB, FZ, ZP * CL), BF), "x_f": ((KF, 32, 128), F32), "x_fb": ((128, 1024), BF),
    "a": ((512, MODES * CH), BF), "m_f": ((KF, 32, 128), F32), "m_fm": ((WD, 16, 128), BF),
    "pt": ((FY // 2, ZP), F32), "pt_m": ((32, 128), BF), "d_f": ((4 * 2 * FX, 128), F32),
    "d_lanes": ((2 * FX, 512), BF), "q_rows": ((2 * GX, 8), F32),
    "q_m": ((WD, 1, 128), F32), "mine": ((128, 128), BF), "cot": ((256, ZP), F32),
    "send_g": ((LV, 64, MODES * CH), BF), "msg_out": ((8, 8, 8, 128), F32),
}
FIRST = ("x_in_f", "z4_f", "tya_f", "x_in_g", "z4_g", "tya_g")


def chain_body(scalars, start, get, res, scr, sem):
    level, wide = here()
    start(FIRST)
    land = {n: scr["land_" + n] for n in LANDS}
    corner = scalars["well_x"][level]
    rows_at = scalars["well_y"][level]
    barrier, count = greet()
    kg, kf = scr["kg"], scr["kf"]
    features(FY, PF, FZ * 4, get("x_in_f"), get("z4_f")[...], get("tya_f")[...], scr["feat_f"], kf, scr["x_ff"])
    features(YG, PG, GZ * 4, get("x_in_g"), get("z4_g")[...], get("tya_g")[...], scr["feat_g"], kg, scr["x_g"])
    pl.semaphore_wait(barrier, count)

    push_level(lambda peer: kg.at[pl.ds(8 * peer, 8)], land["in_level"], sem["in_level"])
    start(CHAIN_INPUTS)
    land["in_level"][level] = kg[pl.ds(8 * level, 8)]
    msg = scr["msg_in"]
    msg[...] = jnp.zeros(msg.shape, F32)
    for w in range(WD):
        msg[w, PG : PG + PF, :] = kf[w // 2]
    finish(land["in_level"], sem["in_level"], LV)
    total = land["in_level"][0] + land["in_level"][1] + land["in_level"][2] + land["in_level"][3]
    for w in range(WD):
        msg[w, :PG, :] = total[w // 8]
    push_wide(lambda peer: msg.at[peer], land["in"], sem["in"])
    land["in"][wide] = msg[wide]
    tile = get("tile")[...]
    lift_g, lift_f = get("lift_g")[...].astype(F32), get("lift_f")[...].astype(F32)
    point_g = mmh(lift_g, get("mix_g")[...].astype(F32))
    point_f = mmh(lift_f, get("mix_f")[...].astype(F32))
    ro_g, ro_f = get("ro_g")[...].astype(F32), get("ro_f")[...].astype(F32)
    spread, fold = get("spread"), get("fold")[...]
    lift_lanes = mm(get("lift_f")[...], spread[...])[4:5, :]
    for b in range(NB):
        scr["lm_g"][b] = point_block(point_g, b, tile, 2)[: GZ * 4]
    w_f, w_g = get("w_f"), get("w_g")
    acc = scr["mix_a"]
    for c in range(CC // CHUNK):
        part = weights_chunk(w_f, c) * lift_lanes[:, CHUNK * c : CHUNK * (c + 1)]
        if c == 0:
            acc[...] = part
        else:
            acc[...] += part
    scr["v_f"][...] = mm_split(acc[...], fold)
    finish(land["in"], sem["in"], WD)

    u = halves(land["in"][...].reshape(WD * 8, 128))
    s = mmh(mmh(get("txs_g")[...], u), selector(lift_g, 2, 2 * lax.rem(wide, 8), 4))
    p_gm = scr["p_gm"]
    p_gm[...] = mix_modes(s, 2, w_g, spread, fold, get("txb_g")[...], scr["mix_ga"], scr["mix_gb"]).reshape(p_gm.shape)
    push_wide(lambda peer: p_gm.at[peer], land["g"], sem["g"])
    land["g"][wide] = p_gm[wide]
    res["s_g"][...] = s
    first = 8 * lax.rem(wide, 2)
    s_f = mmh(mmh(get("txs_f")[...], u), selector(lift_f[:4], 8, first, 4))
    sel_c = selector(lift_f[4:5], 8, first, 1)
    for b in range(NB):
        scr["lm_f"][b] = point_block(point_f[:4], b, tile, 2)
        scr["lc_f"][b] = point_block(point_f[4:5], b, tile, 0)
    finish(land["g"], sem["g"], WD)
    land["g_level"][level] = land["g"][...].reshape(WD * 8, 128).astype(BF)
    push_level(lambda peer: land["g_level"].at[level], land["g_level"], sem["g_level"])
    cot_in = get("cot_in_f")
    for y in range(FY):
        scr["cot_f"][PF * y : PF * (y + 1), :] = cot_in[:, FZ * y : FZ * (y + 1)]
    ones_cl = get("ones_cl")[...]
    scr["wide_cot"][...] = mm_split(scr["cot_f"][...], ones_cl)
    cot, cot_in = scr["cot"], get("cot_in_g")
    cot[...] = jnp.zeros(cot.shape, F32)
    for y in range(YG):
        cot[PG * y : PG * (y + 1), :GZ] = cot_in[:, GZ * y : GZ * (y + 1)]
    finish(land["g_level"], sem["g_level"], LV)

    scr["x_wide"][...] = land["g_level"][...].astype(F32).reshape(KF, 8, 8, 128)
    for q in range(8):
        scr["x_in"][:, 128 * q : 128 * (q + 1)] = scr["x_wide"][:, q].reshape(256, 128).astype(BF)
    perm_in = get("perm_in")[...]
    bb = mm(get("tyi_g")[...], mm(scr["x_in"][...], perm_in).astype(BF)).astype(BF)
    zi = get("zi_g")[...]
    acc, acc_pt = scr["acc"], scr["acc_pt"]
    for b in range(NB):
        pre = block_pre(bb, b, zi) + mm(scr["feat_g"][...], scr["lm_g"][b])
        hidden, slope = gelu_parts(pre)
        scr["slope"][b] = slope.astype(BF)
        part = hidden * lanes_of(ro_g, b, tile)
        if b == 0:
            acc[...] = part
        else:
            acc[...] += part
    sum_cl = get("sum_cl")[...]
    pred = mm_split(acc[...], sum_cl).astype(BF)
    scr["pred_b"][...] = pred
    push_level(lambda peer: scr["pred_b"], land["rows"], sem["rows"])
    land["rows"][level] = pred
    res["pred_g"][...] = pred.astype(F32)
    pick_box = shift_rows(256, LV * 256, 8 * PG * rows_at).astype(BF)
    finish(land["rows"], sem["rows"], LV)

    box = mm(pick_box, land["rows"][...].reshape(LV * 256, ZP))
    a = mmh(box, get("zc")[...])
    scr["s_box"][...] = mmh(get("tya_box")[...], halves(a))
    for p in range(PG):
        for r in range(2):
            at = 2 * MODES * p + MODES * r
            scr["o_box"][:, at : at + MODES] = scr["s_box"][pl.ds(KF * PG * r + p, KF, stride=PG), :]
    spec_m, planes_m = scr["spec_m"], scr["planes_m"]
    spec_m[...] = scr["o_box"][...].reshape(spec_m.shape)
    push_wide(lambda peer: spec_m.at[peer // 2], land["spec"], sem["spec"])
    land["spec"][wide] = spec_m[wide // 2]
    scr["box_f"][...] = box
    planes = [pair_rows(scr["box_f"], p, PG, FY // 4) for p in range(PG)]
    for r in range(PG):
        mine_r = lax.rem(corner + r, PG)
        which = jnp.zeros((32, 128), jnp.int32) + mine_r
        planes_m[r] = sum(jnp.where(which == p, planes[p], 0.0) for p in range(PG)).astype(BF)
    push_wide(lambda peer: planes_m.at[peer % PG], land["box"], sem["box"])
    land["box"][wide] = planes_m[wide % PG]
    pick_x = shift_rows(FX // 2, GX, corner)
    finish(land["spec"], sem["spec"], WD)

    got = land["spec"][...].reshape(WD, 128)
    for p in range(PG):
        scr["x_box"][pl.ds(p, WD, stride=PG), :] = got[:, 2 * MODES * p : 2 * MODES * (p + 1)]
    box = mmh(pick_x, scr["x_box"][...])
    s_f = s_f + mmh(mmh(get("txs_box")[...], halves(box)), sel_c)
    p_f, p_fm = scr["p_f"], scr["p_fm"]
    value = mix_modes(s_f, 8, w_f, spread, fold, get("txb_f")[...], scr["mix_a"], scr["mix_b"])
    for k in range(4):
        p_f[pl.ds(k, 2 * FX, stride=4), :] = value[:, 128 * k : 128 * (k + 1)]
    p_fm[...] = p_f[...].astype(BF).reshape(p_fm.shape)
    push_wide(lambda peer: p_fm.at[peer], land["f"], sem["f"])
    land["f"][wide] = p_fm[wide]
    res["s_f"][...] = s_f
    finish(land["box"], sem["box"], WD)
    plane = pick_plane(land["box"][...].astype(F32), lax.div(corner + wide, PG)).astype(BF)
    rows_up = get("rows_up")
    rows = mm(rows_up[0], plane[:, :ZP]) + mm(rows_up[1], plane[:, ZP:])
    cl = mm(rows.astype(BF), get("z_up")[...]).astype(BF)
    finish(land["f"], sem["f"], WD)

    scr["x_f"][...] = land["f"][...].astype(F32).reshape(KF, 32, 128)
    for g in range(8):
        lanes = scr["x_f"][:, pl.ds(16 * (g // 4) + g % 4, 4, stride=4), :]
        scr["x_fb"][:, 128 * g : 128 * (g + 1)] = lanes.reshape(128, 128).astype(BF)
    bb = mm(get("tyi_f")[...], mm(scr["x_fb"][...], perm_in).astype(BF)).astype(BF)
    zi, zf = get("zi_f")[...], get("zf_f")[...]
    for b in range(NB):
        pre = block_pre(bb, b, zi) + mm(scr["feat_f"][...], scr["lm_f"][b]) + mm(cl, scr["lc_f"][b])
        hidden, slope = gelu_parts(pre)
        ro_lanes = lanes_of(ro_f, b, tile)
        gp = (slope * (scr["wide_cot"][...] * ro_lanes)).astype(BF)
        part = hidden * ro_lanes
        part_pt = gp.astype(F32) * lanes_of(point_f[4:5], b, tile)
        if b == 0:
            acc[...] = part
            acc_pt[...] = part_pt
        else:
            acc[...] += part
            acc_pt[...] += part_pt
        put_block(scr["a"], gp, b, zf)
    z = forward_tail(scr["a"], get("tyf_f")[...], get("perm_wide")[...])
    m_f, m_fm = scr["m_f"], scr["m_fm"]
    for g in range(8):
        m_f[:, pl.ds(16 * (g // 4) + g % 4, 4, stride=4), :] = z[:, 128 * g : 128 * (g + 1)].reshape(KF, 4, 128)
    m_fm[...] = m_f[...].astype(BF).reshape(m_fm.shape)
    push_wide(lambda peer: m_fm.at[peer], land["dual"], sem["dual"])
    land["dual"][wide] = m_fm[wide]
    point = mm_split(acc_pt[...], sum_cl)
    scr["pt"][...] = mmh(mmh(get("rows_down")[...], point), get("z_down")[...])
    pt_m = scr["pt_m"]
    pt_m[...] = pair_rows(scr["pt"], 0, 1, FY // 4).astype(BF)
    push_wide(lambda peer: pt_m, land["pts"], sem["pts"])
    land["pts"][wide] = pt_m[...]
    res["pred_f"][...] = mm_split(acc[...], sum_cl)
    place_x = shift_rows(2 * GX, FX, -2 * corner)
    finish(land["dual"], sem["dual"], WD)

    d_f, d_lanes = scr["d_f"], scr["d_lanes"]
    d_f[...] = land["dual"][...].astype(F32).reshape(d_f.shape)
    for g in range(4):
        d_lanes[:, 128 * g : 128 * (g + 1)] = d_f[pl.ds(g, 2 * FX, stride=4), :].astype(BF)
    z = mm(get("txd_f")[...], d_lanes[...])
    rows = 2 * KF
    zc, zd = z[2 * rows : 3 * rows], z[3 * rows :]
    cols = []
    for m in range(8):
        v = scr["v_f"][rows * m : rows * (m + 1), :]
        lanes = slice(lane_f(m), lane_f(m) + CH)
        cols.append(jnp.concatenate([
            jnp.sum(v * zc[:, lanes], axis=1, keepdims=True),
            jnp.sum(v * zd[:, lanes], axis=1, keepdims=True)], axis=0))
    q_rows, q_m = scr["q_rows"], scr["q_m"]
    q_rows[...] = mmh(place_x, mmh(get("txb_box")[...], jnp.concatenate(cols, axis=1)))
    lanes = [q_rows[pl.ds(r, WD, stride=8), :] for r in range(8)]
    lanes.append(jnp.zeros((WD, 64), F32))
    q_m[...] = jnp.concatenate(lanes, axis=1).reshape(q_m.shape)
    own = land["q"].at[level]
    push_wide(lambda peer: q_m.at[peer], own, sem["q"])
    own[wide] = q_m[wide]
    res["dual_f"][...] = z[: 2 * rows].astype(BF)
    finish(land["pts"], sem["pts"], WD)
    mine = scr["mine"]
    planes = land["pts"][...].astype(F32)
    for p in range(PG):
        mine[32 * p : 32 * (p + 1), :] = pick_plane(planes, PG * wide + p - corner).astype(BF)
    push_level(lambda peer: mine, land["pt_level"], sem["pt_level"])
    land["pt_level"][level] = mine[...]
    finish(own, sem["q"], WD)
    push_level(lambda peer: own, land["q"], sem["q_level"])
    tyb = get("tyb_box")[...]
    tables = []
    for l in range(LV):
        tables.append(mm(shift_rows(YG, FY // 2, YG * level - 8 * scalars["well_y"][l]).astype(BF), tyb).astype(BF))
    finish(land["pt_level"], sem["pt_level"], LV)
    planes = jnp.zeros((128, 128), F32)
    for l in range(LV):
        move = shift_rows(128, 128, 32 * level - 4 * scalars["well_y"][l], 32).astype(BF)
        planes += mm(move, land["pt_level"][l])
    for p in range(PG):
        for k in range(2):
            part = planes[32 * p : 32 * (p + 1), ZP * k : ZP * (k + 1)]
            cot[pl.ds(PG * k + p, 32, stride=2 * PG), :] += part
    finish(land["q"], sem["q_level"], LV)

    q = land["q"][...].reshape(LV * WD, 128)[:, :64]
    odd = jnp.bitwise_and(lax.broadcasted_iota(jnp.int32, q.shape, 0), 1) == 1
    q = jnp.concatenate([jnp.where(odd, 0.0, q), jnp.where(odd, q, 0.0)], axis=1).astype(BF)
    g = mm(q, get("dd_box")[...]).astype(BF)
    total = jnp.zeros((YG, PG * ZP), F32)
    for l in range(LV):
        part = g[WD * l : WD * (l + 1)]
        part = jnp.concatenate([part[:, PG * ZP * k : PG * ZP * (k + 1)] for k in range(4)], axis=0)
        total += mm(tables[l], part)
    for p in range(PG):
        cot[pl.ds(p, YG, stride=PG), :] += total[:, ZP * p : ZP * (p + 1)]
    wide_cot = mm_split(cot[...], ones_cl)
    zf = get("zf_g")[...]
    for b in range(NB):
        gp = (scr["slope"][b].astype(F32) * (wide_cot * lanes_of(ro_g, b, tile))).astype(BF)
        put_block(scr["a"], gp, b, zf)
    send_g = scr["send_g"]
    send_g[...] = forward_tail(scr["a"], get("tyf_g")[...], get("perm_out")[...]).astype(BF).reshape(send_g.shape)
    push_level(lambda peer: send_g.at[peer], land["out_level"], sem["out_level"])
    land["out_level"][level] = send_g[level]
    msg = scr["msg_out"]
    msg[...] = jnp.zeros(msg.shape, F32)
    finish(land["out_level"], sem["out_level"], LV)
    out = land["out_level"]
    total = out[0].astype(F32) + out[1].astype(F32) + out[2].astype(F32) + out[3].astype(F32)
    for q in range(8):
        msg[:, q, :, : 2 * CH] = total[:, 2 * CH * q : 2 * CH * (q + 1)].reshape(8, 8, 2 * CH)
    push_wide(lambda peer: msg.at[peer // 8, peer % 8], res["got_g"], sem["got_g"])
    res["got_g"][wide] = msg[wide // 8, wide % 8]
    finish(res["got_g"], sem["got_g"], WD)


def last_body(scalars, start, get, res, scr, sem):
    start(LAST_INPUTS)
    spread, tile_out = get("spread"), get("tile_out")[...]
    rows = 2 * KF
    done = []

    def send(src, dst, k):
        copy = pltpu.make_async_copy(src, dst, sem["out"].at[k])
        copy.start()
        done.append(copy)

    def grads(s, za, zb, modes, buf):
        sa, sb = stack_modes(s[:rows], modes, lane_g), stack_modes(s[rows:], modes, lane_g)

        def put(lanes, value):
            buf[:, :, :, lanes] = value

        grad_modes(sa, sb, mm(za, tile_out), mm(zb, tile_out), spread, put)

    s_f, d_f = get("s_f")[...], get("dual_f")[...]
    for k in range(2):
        buf = scr["gf"].at[pl.ds(4 * k, 4)]
        d = d_f[:, 256 * k : 256 * (k + 1)]
        grads(s_f[:, 4 * CH * k : 4 * CH * (k + 1)], stack_modes(d[:rows], 4, lane_f), stack_modes(d[rows:], 4, lane_f), 4, buf)
        send(buf, res["grad_f"].at[pl.ds(4 * k, 4)], k)
    z = mm(get("txd_g")[...], get("got_g")[...].reshape(2 * GX, 128).astype(BF))
    grads(get("s_g")[...], stack_modes(z[:rows], 2, lane_f), stack_modes(z[rows:], 2, lane_f), 2, res["grad_g"])
    pred = get("pred_g")
    for y in range(YG):
        scr["out_g"][:, GZ * y : GZ * (y + 1)] = pred[PG * y : PG * (y + 1), :GZ]
    res["coarse"][...] = scr["out_g"][...].astype(BF)
    pred = get("pred_f")
    for y in range(FY):
        scr["out_f"][:, FZ * y : FZ * (y + 1)] = pred[PF * y : PF * (y + 1), :]
    res["fine"][0] = scr["out_f"][...].astype(BF)
    for copy in done:
        copy.wait()


CHAIN_TABLES = {
    "z4_f": Z4_F, "tya_f": TYA_F, "z4_g": Z4_G, "tya_g": TYA_G,
    "tile": TILE_CL, "spread": SPREAD_IN, "fold": FOLD, "txs_g": TXS_G, "txb_g": TXB_G, "txs_f": TXS_F,
    "ones_cl": ONES_CL, "perm_in": PERM_WIDE, "tyi_g": TYI_G, "zi_g": ZI_G, "sum_cl": SUM_CL, "zc": ZC,
    "tya_box": TYA_BOX, "txs_box": TXS_BOX, "txb_f": TXB_F, "rows_up": ROWS_UP, "z_up": Z_UP, "tyi_f": TYI_F,
    "zi_f": ZI_F, "zf_f": ZF_F, "tyf_f": TYF_F, "perm_wide": PERM_WIDE_OUT, "rows_down": ROWS_DOWN, "z_down": Z_DOWN,
    "txd_f": TXD_F, "txb_box": TXB_BOX, "tyb_box": TYB_BOX, "dd_box": DD_BOX, "zf_g": ZF_G, "tyf_g": TYF_G,
    "perm_out": PERM_OUT,
}
CHAIN_PARAMS = ("lift_g", "lift_f", "mix_g", "mix_f", "ro_g", "ro_f", "w_f", "w_g", "cot_in_f", "cot_in_g")
CHAIN_INPUTS = (*CHAIN_PARAMS, *CHAIN_TABLES)
LAST_INPUTS = ("spread", "tile_out", "s_f", "dual_f", "txd_g", "got_g", "s_g", "pred_g", "pred_f")


def shards(coarse_input, fine_input, coarse_cotangent, fine_cotangent, well_x, well_y, coarse_lift, coarse_mixing,
           coarse_spectral, coarse_readout, fine_lift, fine_mixing, fine_spectral, fine_readout):
    inputs = {
        "x_in_f": fine_input[0], "x_in_g": coarse_input, "lift_g": coarse_lift, "lift_f": fine_lift[0],
        "mix_g": coarse_mixing, "mix_f": fine_mixing[0], "ro_g": coarse_readout[None], "ro_f": fine_readout,
        "w_f": fine_spectral[0], "w_g": coarse_spectral, "cot_in_f": fine_cotangent[0], "cot_in_g": coarse_cotangent,
    }
    inputs.update({n: jnp.asarray(t) for n, t in CHAIN_TABLES.items()})
    scratch = {**{"land_" + n: v for n, v in LANDS.items()}, **SCRATCH}
    res = run(chain_body, RESULTS, {"well_x": well_x, "well_y": well_y}, inputs, scratch, SEMS, cid=1, name="chain")
    inputs = {n: res[n] for n in ("s_f", "dual_f", "got_g", "s_g", "pred_g", "pred_f")}
    inputs.update(spread=jnp.asarray(SPREAD_IN), tile_out=jnp.asarray(TILE_OUT), txd_g=jnp.asarray(TXD_G))
    out = run(
        last_body,
        {"grad_g": ((2, KF, 2, CC), F32), "grad_f": ((8, KF, 2, CC), F32), "coarse": ((PG, YG * GZ), BF),
         "fine": ((1, PF, FY * FZ), BF)},
        {}, inputs,
        {"gf": ((8, KF, 2, CC), F32), "out_g": ((PG, YG * GZ), F32), "out_f": ((PF, FY * FZ), F32)},
        ("out",), kept=("grad_f",), name="last")
    return out["coarse"], out["fine"], out["grad_g"], out["grad_f"][None]


def solution(mesh):
    placed = (
        P("wide", "level"),
        P("level", "wide", None),
        P("wide", "level"),
        P("level", "wide", None),
        P(),
        P(),
        P(),
        P(),
        P(("level", "wide"), None, None, None),
        P(),
        P("level", None, None),
        P("level", None, None),
        P("level", "wide", None, None, None),
        P("level", None),
    )
    return jax.shard_map(
        shards,
        mesh=mesh,
        in_specs=placed,
        out_specs=(
            P("wide", "level"),
            P("level", "wide", None),
            P(("level", "wide"), None, None, None),
            P("level", "wide", None, None, None),
        ),
        check_vma=False,
    )
```

```python
import math
from types import SimpleNamespace as Names

import ml_dtypes
import numpy as np
import jax
import jax.numpy as jnp
from jax import lax
from jax.experimental import pallas as pl
from jax.experimental.pallas import tpu as pltpu
from jax.sharding import PartitionSpec as P

MODES = 16
KF = 2 * MODES
CH = 48
NB = 6
CL = 8
GX = 256
GY = 256
GZ = 50
FX = 128
FY = 128
FZ = 64
ZP = 64
LV = 4
WD = 64
PG = 4
YG = 64
PF = 2
CC = CH * CH
BF = jnp.bfloat16
F32 = jnp.float32
HIGH = lax.Precision.HIGHEST
VMEM_BYTES = 60 * 2**20


def bf(x):
    return np.asarray(x, np.float32).astype(ml_dtypes.bfloat16)


def f32(x):
    return np.asarray(x, np.float32)


def waves(rows, length):
    j = np.arange(KF)
    signed = np.where(j < MODES, j, j - KF)
    turn = np.mod(rows[:, None] * signed[None, :], length) * (2.0 * math.pi / length)
    return np.cos(turn) / math.sqrt(length), np.sin(turn) / math.sqrt(length)


def forward_table(rows, length):
    c, s = waves(rows, length)
    c, s = c.T, s.T
    return np.stack([np.stack([c, s], 1), np.stack([-s, c], 1)], 0)


def depth(length):
    c, s = waves(np.arange(length), length)
    both = np.stack([c[:, :MODES], -s[:, :MODES]], 1)
    both = bf(both).astype(np.float64)
    return np.concatenate([both, np.zeros((ZP - length, 2, MODES))], 0)


D_G, D_F = depth(GZ), depth(FZ)
ZMAP = np.zeros((ZP, FZ))
ZMAP[np.arange(FZ) * GZ // FZ, np.arange(FZ)] = 1.0
D_POOL = np.einsum("gf,frk->grk", ZMAP, D_F)


def depth_blocks(d):
    return np.einsum("zrk,ij->zirkj", d, np.eye(CL)).reshape(ZP * CL, 2 * MODES * CL)


def depth_features(d, length):
    return np.einsum("zrk,ij->zirkj", d[:length], np.eye(4)).reshape(length * 4, 2 * MODES * 4)


ZF_G, ZF_F = bf(depth_blocks(D_G)), bf(depth_blocks(D_F))
ZI_G, ZI_F = bf(depth_blocks(D_G).T), bf(depth_blocks(D_F).T)
Z4_G, Z4_F = bf(depth_features(D_G, GZ)), bf(depth_features(D_F, FZ))
ZC = f32(D_POOL.reshape(ZP, 2 * MODES))

FY_G = np.stack([forward_table(v * YG + np.arange(YG), GY) for v in range(LV)], 0)
FY_F = forward_table(np.arange(FY), FY)
FY_BOX = FY_F.reshape(2, KF, 2, FY // 2, 2).sum(4)
FX_G = forward_table(np.arange(GX), GX)
FX_F = forward_table(np.arange(FX), FX)
FX_BOX = FX_F.reshape(2, KF, 2, FX // 2, 2).sum(4)
EYE_G, EYE_F = np.eye(PG), np.eye(PF)

TYA_G = f32(np.einsum("vakbt,pq->vakpbtq", FY_G, EYE_G).reshape(LV, 2 * KF * PG, 2 * YG * PG))
TYA_F = f32(np.einsum("akbt,pq->akpbtq", FY_F, EYE_F).reshape(2 * KF * PF, 2 * FY * PF))
TYA_BOX = f32(np.einsum("akbt,pq->akpbtq", FY_BOX, EYE_G).reshape(2 * KF * PG, FY * PG))
TYF_G = bf(np.einsum("vakbt,pq->vkpabtq", FY_G, EYE_G).reshape(LV, KF * PG * 2, 2 * YG * PG))
TYF_F = bf(np.einsum("akbt,pq->kpabtq", FY_F, EYE_F).reshape(KF * PF * 2, 2 * FY * PF))
TYI_G = bf(np.einsum("vbkat,pq->vatpkqb", FY_G, EYE_G).reshape(LV, 2 * YG * PG, KF * PG * 2))
TYI_F = bf(np.einsum("bkat,pq->atpkqb", FY_F, EYE_F).reshape(2 * FY * PF, KF * PF * 2))
TYB_BOX = bf(np.repeat(FY_BOX.transpose(3, 2, 0, 1).reshape(FY // 2, 4 * KF), 2, axis=1))
DD_BOX = bf(np.einsum("zahk,pq,rs->hprkasqz", D_POOL.reshape(ZP, 2, 2, 8), EYE_G, np.eye(2)).reshape(128, 4 * PG * ZP))


def source_rows(table):
    a = np.stack([table[0], -table[1]], 1)
    b = np.stack([table[1], table[0]], 1)
    return np.stack([a, b], 0).reshape(4 * KF, 2, -1)


def in_rows(table, planes, first):
    rows = source_rows(table).reshape(4 * KF, 2, WD, planes)
    out = np.zeros((4 * KF, 2, WD, 8))
    out[..., first : first + planes] = rows
    return out.reshape(4 * KF, 2 * WD * 8)


TXS_G = f32(in_rows(FX_G, PG, 0))
TXS_F = f32(in_rows(FX_F, PF, PG))
TXS_BOX = f32(source_rows(FX_BOX).reshape(4 * KF, FX))


def dual_rows(table, count):
    r, i = table[0], table[1]
    kinds = [np.stack([r, r], 1), np.stack([i, i], 1), np.stack([r, i], 1), np.stack([i, -r], 1)]
    rows = np.stack(kinds[:count], 0).transpose(0, 1, 2, 4, 3)
    return rows.reshape(count * 2 * KF, -1)


TXD_G = bf(dual_rows(FX_G, 2))
TXD_F = bf(dual_rows(FX_F, 4))


def back_rows(table):
    back = table.transpose(3, 2, 0, 1)
    back = np.stack([back, back], 4)
    return back.reshape(back.shape[0] * 2, 4 * KF)


TXB_G = bf(back_rows(FX_G))
TXB_F = bf(back_rows(FX_F))
TXB_BOX = f32(back_rows(FX_BOX))

PERM = np.zeros((MODES, NB, CL, NB, MODES, CL))
for _k in range(MODES):
    for _b in range(NB):
        for _l in range(CL):
            PERM[_k, _b, _l, _b, _k, _l] = 1.0
PERM = PERM.reshape(MODES * CH, MODES * CH)
PERM_OUT = bf(PERM.T)
PERM_WIDE = np.zeros((8, 128, MODES * CH))
PERM_WIDE[:, : 2 * CH] = PERM.reshape(8, 2 * CH, MODES * CH)
PERM_WIDE = PERM_WIDE.reshape(1024, MODES * CH)
PERM_WIDE, PERM_WIDE_OUT = bf(PERM_WIDE), bf(PERM_WIDE.T)
SPREAD_IN = bf(np.kron(np.eye(CH), np.ones((1, CH))))
CHUNK = 8 * CH
TILE_OUT = bf(np.kron(np.ones((1, 8)), np.eye(CH)))
FOLD = bf(np.kron(np.ones((8, 1)), np.eye(CH)))
ONES_CL = bf(np.kron(np.eye(ZP), np.ones((1, CL))))
SUM_CL = bf(np.kron(np.eye(ZP), np.ones((CL, 1))))
TILE_CL = f32(np.kron(np.ones((1, ZP)), np.eye(CL)))
ROWS_UP = np.kron(np.eye(FY // 2), np.ones((2 * PF, 1))).reshape(256, FY // 4, 2).transpose(2, 0, 1)
ROWS_UP = bf(ROWS_UP)
ROWS_DOWN = f32(np.kron(np.eye(FY // 2), np.ones((1, 2 * PF))))
Z_UP = bf(ZMAP)
Z_DOWN = f32(ZMAP.T)


def mm(a, b):
    return jnp.dot(a, b, preferred_element_type=F32)


def mmh(a, b):
    return jnp.dot(a, b, preferred_element_type=F32, precision=HIGH)


MESH = pl.DeviceIdType.MESH
DMA2 = pltpu.SemaphoreType.DMA((2,))


def vm(shape, kind=F32):
    return pltpu.VMEM(shape, kind)


BY_LEVEL = dict(tya_g=LV, tyi_g=LV, tyf_g=LV)


def run(body, outs, smem, inputs, scratch, sems={}, kept=0, passed=(), cid=None, name=None):
    held = {n: vm(t.shape[1:] if n in BY_LEVEL else t.shape, t.dtype) for n, t in inputs.items() if n not in passed}

    def kernel(*refs):
        refs = list(refs)

        def take(names):
            got = {n: refs.pop(0) for n in names}
            return got

        scalars = take(smem)
        given = take(inputs)
        res = take(outs)
        scr = take(scratch)
        sem = take(sems)
        inside = take(held)
        load_sem = refs.pop(0)
        level = lax.axis_index("level")
        copies, started, ready = {}, set(), set()
        for k, n in enumerate(held):
            src = given[n].at[level] if n in BY_LEVEL else given[n]
            copies[n] = pltpu.make_async_copy(src, inside[n], load_sem.at[k])

        def start(count):
            for n in list(copies)[:count]:
                if n not in started:
                    copies[n].start()
                    started.add(n)

        class Get:
            def __getattr__(self, n):
                if n in passed:
                    return given[n]
                if n not in ready:
                    copies[n].wait()
                    ready.add(n)
                return inside[n]

        body(Names(**scalars), start, Get(), Names(**res), Names(**scr), Names(**sem))

    got = pl.pallas_call(
        kernel,
        out_shape=[jax.ShapeDtypeStruct(s, d) for s, d in outs.values()],
        in_specs=[pl.BlockSpec(memory_space=pltpu.SMEM)] * len(smem) + [pl.BlockSpec(memory_space=pl.ANY)] * len(inputs),
        out_specs=[pl.BlockSpec(memory_space=pl.ANY if k < kept else pltpu.VMEM) for k in range(len(outs))],
        scratch_shapes=[pltpu.SemaphoreType.DMA((v,)) if v == 4 else vm(*v) for v in scratch.values()] + [DMA2] * len(sems) + list(held.values())
        + [pltpu.SemaphoreType.DMA((len(held),))],
        name=name,
        compiler_params=pltpu.CompilerParams(
            vmem_limit_bytes=VMEM_BYTES, collective_id=cid, has_side_effects=cid is not None),
    )(*smem.values(), *inputs.values())
    return Names(**dict(zip(outs, got)))


def halves(u):
    half = u.shape[1] // 2
    return jnp.concatenate([u[:, :half], u[:, half:]], axis=0)


def features(rows, planes, width, x_ref, z, table, feat_ref, out_ref, scr):
    for y in range(rows):
        scr[planes * y : planes * (y + 1), :] = x_ref[:, width * y : width * (y + 1)].astype(F32)
    feat = scr[...].astype(BF)
    feat_ref[...] = feat
    both = mmh(table, halves(mm(feat, z)))
    rows_out = both.shape[0] // 2
    lanes = jnp.concatenate([both[:rows_out], both[rows_out:]], axis=1)
    out_ref[...] = lanes.reshape(out_ref.shape)


def lanes_of_modes(shape):
    lane = lax.broadcasted_iota(jnp.int32, shape, 1)
    inside = jnp.bitwise_and(lane, 127)
    mode = 2 * lax.shift_right_logical(lane, 7) + (inside >= CH).astype(jnp.int32)
    return jnp.where(inside < 2 * CH, mode, 8 + MODES)


def stack_modes(x, modes, lane):
    return jnp.concatenate([x[:, lane(m) : lane(m) + CH] for m in range(modes)], axis=0)


def lane_g(m):
    return CH * m


def lane_f(m):
    return 128 * (m // 2) + CH * (m % 2)


def weights_chunk(w_ref, c):
    w = w_ref[:, :, :, CHUNK * c : CHUNK * (c + 1)].astype(F32)
    return w.reshape(w.shape[0] * 2 * KF, CHUNK)


def mix_modes(s, modes, w_ref, spread, fold, table, acc_a, acc_b):
    half = 2 * KF
    sa, sb = stack_modes(s[:half], modes, lane_g), stack_modes(s[half:], modes, lane_g)
    for c in range(CC // CHUNK):
        w = weights_chunk(w_ref, c)
        e = spread[:, CHUNK * c : CHUNK * (c + 1)]
        if c == 0:
            acc_a[...] = w * mm_split(sa, e)
            acc_b[...] = w * mm_split(sb, e)
        else:
            acc_a[...] += w * mm_split(sa, e)
            acc_b[...] += w * mm_split(sb, e)
    pa, pb = mm_split(acc_a[...], fold), mm_split(acc_b[...], fold)
    spare = jnp.zeros((2 * half, 128 - 2 * CH), F32)
    parts = []
    for m in range(modes):
        parts.append(jnp.concatenate([pa[half * m : half * (m + 1)], pb[half * m : half * (m + 1)]], axis=0))
        if m % 2 == 1:
            parts.append(spare)
    return mm_split_right(table, jnp.concatenate(parts, axis=1))


def grad_modes(sa, sb, za, zb, spread, put):
    for c in range(CC // CHUNK):
        e = spread[:, CHUNK * c : CHUNK * (c + 1)]
        g = mm_split(sa, e) * za + mm_split(sb, e) * zb
        put(slice(CHUNK * c, CHUNK * (c + 1)), g.reshape(g.shape[0] // (2 * KF), KF, 2, CHUNK))


def grads(s, za, zb, modes, spread, tile_out, buf):
    rows = 2 * KF
    sa, sb = stack_modes(s[:rows], modes, lane_g), stack_modes(s[rows:], modes, lane_g)

    def put(lanes, value):
        buf[:, :, :, lanes] = value

    grad_modes(sa, sb, mm_split(za, tile_out), mm_split(zb, tile_out), spread, put)


def shift_rows(rows, cols, by, group_rows=None):
    r = lax.broadcasted_iota(jnp.int32, (rows, cols), 0)
    c = lax.broadcasted_iota(jnp.int32, (rows, cols), 1)
    hit = c - r == by
    if group_rows is not None:
        shift = group_rows.bit_length() - 1
        hit = jnp.logical_and(hit, lax.shift_right_logical(r, shift) == lax.shift_right_logical(c, shift))
    return jnp.where(hit, 1.0, 0.0)


def pick_packed(by, half):
    r = lax.broadcasted_iota(jnp.int32, (256, LV * 128), 0)
    c = lax.broadcasted_iota(jnp.int32, (256, LV * 128), 1)
    row = 256 * lax.shift_right_logical(c, 7) + jnp.bitwise_and(c, 127) + 128 * half
    return jnp.where(row - r == by, 1.0, 0.0).astype(BF)


def where_at(which, at, planes):
    return jnp.where(which == at, planes, 0.0)


def pick_plane(planes, at):
    which = lax.broadcasted_iota(jnp.int32, planes.shape, 0)
    return jnp.sum(jnp.where(which == at, planes, 0.0), axis=0)


def pair_rows(scr, first, stride, count):
    even = scr[pl.ds(first, count, stride=2 * stride), :]
    odd = scr[pl.ds(first + stride, count, stride=2 * stride), :]
    return jnp.concatenate([even, odd], axis=1)


def selector(lift, count, first, features_in):
    shape = (MODES * features_in, count * CH)
    rows = lax.broadcasted_iota(jnp.int32, shape, 0)
    cols = lax.broadcasted_iota(jnp.int32, shape, 1)
    tiled = jnp.concatenate([lift] * MODES, axis=0) if features_in > 1 else lift
    tiled = jnp.concatenate([tiled] * count, axis=1)
    mode = sum((cols >= CH * m).astype(jnp.int32) for m in range(1, count))
    kz = lax.shift_right_logical(rows, 2) if features_in > 1 else rows
    return jnp.where(kz == first + mode, tiled, 0.0)


K0 = math.sqrt(2.0 / math.pi)


def gelu_parts(x):
    x2 = x * x
    half = 0.5 + 0.5 * jnp.tanh(x * (K0 + (0.044715 * K0) * x2))
    slope = half + x * (2.0 * K0 + (6.0 * 0.044715 * K0) * x2) * (half - half * half)
    return x * half, slope


def block_pre(bb, b, zi):
    rows = bb.shape[0] // 2
    lanes = slice(MODES * CL * b, MODES * CL * (b + 1))
    return mm(bb[:rows, lanes], zi[: MODES * CL]) + mm(bb[rows:, lanes], zi[MODES * CL :])


def lanes_of(row, b, tile):
    return mmh(row[:, CL * b : CL * (b + 1)], tile)


def point_block(point, b, tile, shift):
    count = point.shape[0]
    full = jnp.concatenate([lanes_of(point, b, tile)] * ZP, axis=0)
    z_row = lax.shift_right_logical(lax.broadcasted_iota(jnp.int32, full.shape, 0), shift)
    z_col = lax.shift_right_logical(lax.broadcasted_iota(jnp.int32, full.shape, 1), 3)
    return jnp.where(z_row == z_col, full, 0.0).astype(BF)


def split(x):
    top = x.astype(BF)
    return top, (x - top.astype(F32)).astype(BF)


def mm_split(x, table):
    top, low = split(x)
    return mm(top, table) + mm(low, table)


def mm_split_right(table, x):
    top, low = split(x)
    return mm(table, top) + mm(table, low)


def put_block(a_scr, gp, b, zf):
    a = mm(gp, zf).astype(BF)
    rows = a.shape[0]
    width = MODES * CL
    a_scr[:rows, width * b : width * (b + 1)] = a[:, :width]
    a_scr[rows:, width * b : width * (b + 1)] = a[:, width:]


def forward_tail(a_scr, table, perm):
    return mm(mm(table, a_scr[...]).astype(BF), perm)


def here():
    return lax.axis_index("level"), lax.axis_index("wide")


def greet():
    level, wide = here()
    barrier = pltpu.get_barrier_semaphore()
    for i in range(1, LV):
        pl.semaphore_signal(barrier, inc=1, device_id=(lax.rem(level + i, LV), wide), device_id_type=MESH)

    def one(i, carry):
        pl.semaphore_signal(barrier, inc=1, device_id=(level, lax.rem(wide + i, WD)), device_id_type=MESH)
        return carry

    lax.fori_loop(1, WD, one, 0)
    return barrier, LV - 1 + WD - 1


def remote(src, dst, sems, to):
    return pltpu.make_async_remote_copy(
        src_ref=src, dst_ref=dst, send_sem=sems.at[0], recv_sem=sems.at[1], device_id=to, device_id_type=MESH)


def push_wide(source, land, sems):
    level, wide = here()

    def one(i, carry):
        peer = lax.rem(wide + i, WD)
        remote(source(peer), land.at[wide], sems, (level, peer)).start()
        return carry

    lax.fori_loop(1, WD, one, 0)


def push_level(source, land, sems):
    level, wide = here()
    for i in range(1, LV):
        peer = lax.rem(level + i, LV)
        remote(source(peer), land.at[level], sems, (peer, wide)).start()


def push_y(source, land, sems):
    level, wide = here()
    for i in range(1, 4):
        peer = lax.rem(wide + 16 * i, WD)
        remote(source, land.at[wide // 16], sems, (level, peer)).start()


def push_zc(source, land, sems):
    level, wide = here()
    base = 16 * (wide // 16)

    def one(i, carry):
        peer = lax.rem(wide + i, 16)
        remote(source(peer), land.at[wide % 16], sems, (level, base + peer)).start()
        return carry

    lax.fori_loop(1, 16, one, 0)


def finish(land, sems, count):
    level, wide = here()
    part = land.at[pl.ds(0, count - 1)]
    done = remote(part, part, sems, (level, wide))
    done.wait_send()
    done.wait_recv()


SEMS = dict(
    in_level=2, inw=2, g=2, g_level=2, rows=2, spec=2, box1=2, box2=2, f=2, dual=2, pt1=2, pt2=2, q=2, q_level=2,
    pt_level=2, out_level=2, got_g=2, out=2,
)
RESULTS = dict(
    grad_f=((8, KF, 2, CC), F32), s_g=((4 * KF, 2 * CH), F32), got_g=((WD, 8, 128), BF),
    coarse=((PG, YG * GZ), BF), fine=((1, PF, FY * FZ), BF),
)
LANDS = dict(
    in_level=((LV, 8, PG, 128), F32), inw=((WD, 8, 128), BF),
    g=((LV, WD, 8, 128), BF), rows=((LV, 128, 128), BF), spec=((WD, 1, 128), F32),
    box1=((4, PG, 32, 128), BF), box2=((16, 32, 128), BF), f=((WD, 16, 128), BF), dual=((WD, 16, 128), BF), pt1=((16, 32, 128), BF), pt2=((4, PG, 32, 128), BF),
    q=((LV, WD, 1, 128), F32), pt_level=((LV, 128, 128), BF), out_level=((LV, 64, MODES * CH), BF),
)
LANDED = "_land"
SCRATCH = dict(
    x_g=((256, GZ * 4), F32), x_ff=((256, FZ * 4), F32), feat_g=((256, GZ * 4), BF), feat_f=((256, FZ * 4), BF),
    kg=((KF, PG, 128), F32), kf=((KF, PF, 128), F32), cot_f=((256, FZ), F32),
    msg_in=((WD, 8, 128), F32), msg_b=((WD, 8, 128), BF), p_gm=((WD, 8, 128), BF), mix_a=((512, CHUNK), F32), mix_b=((512, CHUNK), F32),
    mix_ga=((128, CHUNK), F32), mix_gb=((128, CHUNK), F32), wide_cot=((256, ZP * CL), F32),
    x_wide=((KF, 8, 8, 128), F32), x_in=((256, 1024), BF), acc=((256, ZP * CL), F32),
    acc_pt=((256, ZP * CL), F32), slope=((NB, 256, ZP * CL), BF), pred_b=((128, 128), BF), pred_g=((256, ZP), F32), pred_f=((256, FZ), F32),
    box_f=((256, ZP), F32), s_box=((2 * KF * PG, MODES), F32),
    o_box=((KF, 128), F32), spec_m=((KF, 1, 128), F32), planes_m=((PG, 32, 128), BF),
    x_box=((GX, 2 * MODES), F32), p_f=((4 * 2 * FX, 128), F32), p_fm=((WD, 16, 128), BF),
    v_f=((8 * 2 * KF, CH), F32), pre_g=((NB, 256, ZP * CL), F32), pre_f=((NB, 256, ZP * CL), F32),
    pre_p=((2 * FX, 512), F32), v_lanes=((2 * KF, 512), F32), s_f=((4 * KF, 8 * CH), F32), dual_f=((4 * KF, 512), F32), x_f=((KF, 32, 128), F32), x_fb=((128, 1024), BF),
    a=((512, MODES * CH), BF), m_f=((KF, 32, 128), F32), m_fm=((WD, 16, 128), BF),
    pt=((FY // 2, ZP), F32), pt_m=((32, 128), BF), d_f=((4 * 2 * FX, 128), F32),
    d_lanes=((2 * FX, 512), BF), q_rows=((2 * GX, 8), F32),
    q_m=((WD, 1, 128), F32), mine=((128, 128), BF), box_m=((16, 32, 128), BF), pt_mid=((PG, 32, 128), BF), gf=((8, KF, 2, CC), F32), cot=((256, ZP), F32),
    send_g=((LV, 64, MODES * CH), BF), msg_out=((8, 8, 8, 128), F32), msg_ob=((8, 8, 8, 128), BF), out_g=((PG, YG * GZ), F32), out_f=((PF, FY * FZ), F32),
)

def chain_body(scalars, start, get, res, scr, sem):
    level, wide = here()
    start(6)
    land = Names(**{n: getattr(scr, n + LANDED) for n in LANDS})
    corner = scalars.well_x[level]
    rows_at = scalars.well_y[level]
    barrier, count = greet()
    kg, kf = scr.kg, scr.kf
    features(FY, PF, FZ * 4, get.x_in_f, get.z4_f[...], get.tya_f[...], scr.feat_f, kf, scr.x_ff)
    features(YG, PG, GZ * 4, get.x_in_g, get.z4_g[...], get.tya_g[...], scr.feat_g, kg, scr.x_g)
    pl.semaphore_wait(barrier, count)

    push_level(lambda peer: kg.at[pl.ds(8 * peer, 8)], land.in_level, sem.in_level)
    start(None)
    land.in_level[level] = kg[pl.ds(8 * level, 8)]
    msg = scr.msg_in
    msg[...] = jnp.zeros(msg.shape, F32)
    for w in range(WD):
        msg[w, PG : PG + PF, :] = kf[w // 2]
    finish(land.in_level, sem.in_level, LV)
    total = land.in_level[0] + land.in_level[1] + land.in_level[2] + land.in_level[3]
    for w in range(WD):
        msg[w, :PG, :] = total[w // 8]
    msg_b = scr.msg_b
    msg_b[...] = msg[...].astype(BF)
    push_wide(lambda peer: msg_b.at[peer], land.inw, sem.inw)
    land.inw[wide] = msg_b[wide]
    tile = get.tile[...]
    lift_g, lift_f = get.lift_g[...].astype(F32), get.lift_f[...].astype(F32)
    point_g = mmh(lift_g, get.mix_g[...].astype(F32))
    point_f = mmh(lift_f, get.mix_f[...].astype(F32))
    ro_g, ro_f = get.ro_g[...].astype(F32), get.ro_f[...].astype(F32)
    spread, fold = get.spread, get.fold[...]
    lift_lanes = mm(get.lift_f[...], spread[...])[4:5, :]
    ro_gl = [lanes_of(ro_g, b, tile) for b in range(NB)]
    ro_fl = [lanes_of(ro_f, b, tile) for b in range(NB)]
    v_fl = [lanes_of(point_f[4:5], b, tile) for b in range(NB)]
    for b in range(NB):
        scr.pre_g[b] = mm(scr.feat_g[...], point_block(point_g, b, tile, 2)[: GZ * 4])
    w_f, w_g = get.w_f, get.w_g
    acc = scr.mix_a
    for c in range(CC // CHUNK):
        part = weights_chunk(w_f, c) * lift_lanes[:, CHUNK * c : CHUNK * (c + 1)]
        if c == 0:
            acc[...] = part
        else:
            acc[...] += part
    scr.v_f[...] = mm_split(acc[...], fold)
    scr.v_lanes[...] = jnp.zeros(scr.v_lanes.shape, F32)
    for m in range(8):
        scr.v_lanes[:, lane_f(m) : lane_f(m) + CH] = scr.v_f[2 * KF * m : 2 * KF * (m + 1), :]
    finish(land.inw, sem.inw, WD)

    u = halves(land.inw[...].astype(F32).reshape(WD * 8, 128))
    s = mmh(mmh(get.txs_g[...], u), selector(lift_g, 2, 2 * lax.rem(wide, 8), 4))
    p_gm = scr.p_gm
    p_gm_rows = mix_modes(s, 2, w_g, spread, fold, get.txb_g[...], scr.mix_ga, scr.mix_gb)
    p_gm[...] = p_gm_rows.reshape(p_gm.shape).astype(BF)
    own_g = land.g.at[level]
    push_wide(lambda peer: p_gm.at[peer], own_g, sem.g)
    own_g[wide] = p_gm[wide]
    res.s_g[...] = s
    first = 8 * lax.rem(wide, 2)
    s_f = mmh(mmh(get.txs_f[...], u), selector(lift_f[:4], 8, first, 4))
    finish(own_g, sem.g, WD)
    push_level(lambda peer: own_g, land.g, sem.g_level)
    scr.pre_p[...] = mix_modes(s_f, 8, w_f, spread, fold, get.txb_f[...], scr.mix_a, scr.mix_b)
    sel_c = selector(lift_f[4:5], 8, first, 1)
    sel_u = lax.broadcasted_iota(jnp.int32, (MODES, 512), 0) == first + lanes_of_modes((MODES, 512))
    sel_u = jnp.where(sel_u, 1.0, 0.0)
    for b in range(NB):
        scr.pre_f[b] = mm(scr.feat_f[...], point_block(point_f[:4], b, tile, 2))
    cot_in = get.cot_in_f
    for y in range(FY):
        scr.cot_f[PF * y : PF * (y + 1), :] = cot_in[:, FZ * y : FZ * (y + 1)]
    ones_cl = get.ones_cl[...]
    scr.wide_cot[...] = mm_split(scr.cot_f[...], ones_cl)
    cot, cot_in = scr.cot, get.cot_in_g
    cot[...] = jnp.zeros(cot.shape, F32)
    for y in range(YG):
        cot[PG * y : PG * (y + 1), :GZ] = cot_in[:, GZ * y : GZ * (y + 1)]
    finish(land.g, sem.g_level, LV)

    scr.x_wide[...] = land.g[...].astype(F32).reshape(KF, 8, 8, 128)
    for q in range(8):
        scr.x_in[:, 128 * q : 128 * (q + 1)] = scr.x_wide[:, q].reshape(256, 128).astype(BF)
    perm_in = get.perm_in[...]
    bb = mm(get.tyi_g[...], mm(scr.x_in[...], perm_in).astype(BF)).astype(BF)
    zi = get.zi_g[...]
    acc, acc_pt = scr.acc, scr.acc_pt
    for b in range(NB):
        pre = block_pre(bb, b, zi) + scr.pre_g[b]
        hidden, slope = gelu_parts(pre)
        scr.slope[b] = slope.astype(BF)
        part = hidden * ro_gl[b]
        if b == 0:
            acc[...] = part
        else:
            acc[...] += part
    sum_cl = get.sum_cl[...]
    pred = mm_split(acc[...], sum_cl)
    scr.pred_b[...] = jnp.concatenate([pred[:128], pred[128:]], axis=1).astype(BF)
    push_level(lambda peer: scr.pred_b, land.rows, sem.rows)
    land.rows[level] = scr.pred_b[...]
    scr.pred_g[...] = pred
    pick_box = [pick_packed(8 * PG * rows_at, h) for h in range(2)]
    finish(land.rows, sem.rows, LV)

    rows = land.rows[...].reshape(LV * 128, 128)
    box = mm(pick_box[0], rows[:, :ZP]) + mm(pick_box[1], rows[:, ZP:])
    a = mmh(box, get.zc[...])
    scr.s_box[...] = mmh(get.tya_box[...], halves(a))
    for p in range(PG):
        for r in range(2):
            at = 2 * MODES * p + MODES * r
            scr.o_box[:, at : at + MODES] = scr.s_box[pl.ds(KF * PG * r + p, KF, stride=PG), :]
    spec_m, planes_m = scr.spec_m, scr.planes_m
    spec_m[...] = scr.o_box[...].reshape(spec_m.shape)
    push_wide(lambda peer: spec_m.at[peer // 2], land.spec, sem.spec)
    land.spec[wide] = spec_m[wide // 2]
    scr.box_f[...] = box
    for p in range(PG):
        planes_m[p] = pair_rows(scr.box_f, p, PG, FY // 4).astype(BF)
    push_y(planes_m, land.box1, sem.box1)
    y_me, zc_me = wide // 16, wide % 16
    land.box1[y_me] = planes_m[...]
    pick_x = shift_rows(FX // 2, GX, corner)
    txs_box = get.txs_box[...]
    txs_box = jnp.concatenate([mmh(txs_box[:, : FX // 2], pick_x), mmh(txs_box[:, FX // 2 :], pick_x)], axis=1)
    vv = jnp.concatenate([scr.v_lanes[...]] * 2, axis=0)
    finish(land.box1, sem.box1, 4)
    which = lax.broadcasted_iota(jnp.int32, (16, 32, 128), 0) + 16 * y_me
    box_m = jnp.zeros((16, 32, 128), F32)
    for p in range(PG):
        plane = jnp.zeros((32, 128), F32)
        for y in range(4):
            at = 64 * y + 4 * zc_me + p - corner
            inside = jnp.logical_and(at >= 0, at < WD).astype(jnp.int32)
            plane += where_at(jnp.zeros((32, 128), jnp.int32) + inside, 1, land.box1[y, p].astype(F32))
        box_m += where_at(which, lax.rem(4 * zc_me + p - corner + 4 * WD, WD), plane[None])
    scr.box_m[...] = box_m.astype(BF)
    push_zc(lambda peer: scr.box_m.at[peer], land.box2, sem.box2)
    land.box2[zc_me] = scr.box_m[zc_me]
    finish(land.spec, sem.spec, WD)

    got = land.spec[...].reshape(WD, 128)
    for p in range(PG):
        scr.x_box[pl.ds(p, WD, stride=PG), :] = got[:, 2 * MODES * p : 2 * MODES * (p + 1)]
    uc = mmh(txs_box, halves(scr.x_box[...]))
    value = scr.pre_p[...] + mm_split_right(get.txb_f[...], mmh(uc, sel_u) * vv)
    p_f, p_fm = scr.p_f, scr.p_fm
    for k in range(4):
        p_f[pl.ds(k, 2 * FX, stride=4), :] = value[:, 128 * k : 128 * (k + 1)]
    p_fm[...] = p_f[...].astype(BF).reshape(p_fm.shape)
    push_wide(lambda peer: p_fm.at[peer], land.f, sem.f)
    land.f[wide] = p_fm[wide]
    scr.s_f[...] = s_f + mmh(uc, sel_c)
    lc_f = [point_block(point_f[4:5], b, tile, 0) for b in range(NB)]
    finish(land.box2, sem.box2, 16)
    plane = jnp.sum(land.box2[...].astype(F32), axis=0).astype(BF)
    rows_up = get.rows_up
    rows = mm(rows_up[0], plane[:, :ZP]) + mm(rows_up[1], plane[:, ZP:])
    cl = mm(rows.astype(BF), get.z_up[...]).astype(BF)
    for b in range(NB):
        scr.pre_f[b] += mm(cl, lc_f[b])
    finish(land.f, sem.f, WD)

    scr.x_f[...] = land.f[...].astype(F32).reshape(KF, 32, 128)
    for g in range(8):
        lanes = scr.x_f[:, pl.ds(16 * (g // 4) + g % 4, 4, stride=4), :]
        scr.x_fb[:, 128 * g : 128 * (g + 1)] = lanes.reshape(128, 128).astype(BF)
    bb = mm(get.tyi_f[...], mm(scr.x_fb[...], perm_in).astype(BF)).astype(BF)
    zi, zf = get.zi_f[...], get.zf_f[...]
    for b in range(NB):
        pre = block_pre(bb, b, zi) + scr.pre_f[b]
        hidden, slope = gelu_parts(pre)
        ro_lanes = ro_fl[b]
        gp = (slope * (scr.wide_cot[...] * ro_lanes)).astype(BF)
        part = hidden * ro_lanes
        part_pt = gp.astype(F32) * v_fl[b]
        if b == 0:
            acc[...] = part
            acc_pt[...] = part_pt
        else:
            acc[...] += part
            acc_pt[...] += part_pt
        put_block(scr.a, gp, b, zf)
    z = forward_tail(scr.a, get.tyf_f[...], get.perm_wide[...])
    m_f, m_fm = scr.m_f, scr.m_fm
    for g in range(8):
        m_f[:, pl.ds(16 * (g // 4) + g % 4, 4, stride=4), :] = z[:, 128 * g : 128 * (g + 1)].reshape(KF, 4, 128)
    m_fm[...] = m_f[...].astype(BF).reshape(m_fm.shape)
    push_wide(lambda peer: m_fm.at[peer], land.dual, sem.dual)
    land.dual[wide] = m_fm[wide]
    point = mm_split(acc_pt[...], sum_cl)
    scr.pt[...] = mmh(mmh(get.rows_down[...], point), get.z_down[...])
    pt_m = scr.pt_m
    pt_m[...] = pair_rows(scr.pt, 0, 1, FY // 4).astype(BF)
    push_zc(lambda peer: pt_m, land.pt1, sem.pt1)
    land.pt1[zc_me] = pt_m[...]
    scr.pred_f[...] = mm_split(acc[...], sum_cl)
    place_x = mmh(shift_rows(2 * GX, FX, -2 * corner), get.txb_box[...])
    which = lax.broadcasted_iota(jnp.int32, (16, 32, 128), 0)
    finish(land.pt1, sem.pt1, 16)
    planes = land.pt1[...].astype(F32)
    for p in range(PG):
        at = lax.rem(4 * zc_me + p - corner - 16 * y_me + 8 * WD, WD)
        scr.pt_mid[p] = jnp.sum(where_at(which, at, planes), axis=0).astype(BF)
    push_y(scr.pt_mid, land.pt2, sem.pt2)
    land.pt2[y_me] = scr.pt_mid[...]
    finish(land.dual, sem.dual, WD)

    d_f, d_lanes = scr.d_f, scr.d_lanes
    d_f[...] = land.dual[...].astype(F32).reshape(d_f.shape)
    for g in range(4):
        d_lanes[:, 128 * g : 128 * (g + 1)] = d_f[pl.ds(g, 2 * FX, stride=4), :].astype(BF)
    z = mm(get.txd_f[...], d_lanes[...])
    rows = 2 * KF
    zc, zd = z[2 * rows : 3 * rows], z[3 * rows :]
    cols = []
    for m in range(8):
        v = scr.v_f[rows * m : rows * (m + 1), :]
        lanes = slice(lane_f(m), lane_f(m) + CH)
        cols.append(jnp.concatenate([
            jnp.sum(v * zc[:, lanes], axis=1, keepdims=True),
            jnp.sum(v * zd[:, lanes], axis=1, keepdims=True)], axis=0))
    q_rows, q_m = scr.q_rows, scr.q_m
    q_rows[...] = mmh(place_x, jnp.concatenate(cols, axis=1))
    lanes = [q_rows[pl.ds(r, WD, stride=8), :] for r in range(8)]
    lanes.append(jnp.zeros((WD, 64), F32))
    q_m[...] = jnp.concatenate(lanes, axis=1).reshape(q_m.shape)
    own = land.q.at[level]
    push_wide(lambda peer: q_m.at[peer], own, sem.q)
    own[wide] = q_m[wide]
    scr.dual_f[...] = z[: 2 * rows]
    finish(land.pt2, sem.pt2, 4)
    mine = scr.mine
    which = lax.broadcasted_iota(jnp.int32, (4, 32, 128), 0)
    for p in range(PG):
        at = PG * wide + p - corner
        at = jnp.where(jnp.logical_and(at >= 0, at < WD), lax.shift_right_logical(at, 4), 4)
        planes = where_at(which, at, land.pt2[:, p].astype(F32))
        mine[32 * p : 32 * (p + 1), :] = jnp.sum(planes, axis=0).astype(BF)
    push_level(lambda peer: mine, land.pt_level, sem.pt_level)
    land.pt_level[level] = mine[...]
    finish(own, sem.q, WD)
    push_level(lambda peer: own, land.q, sem.q_level)
    tyb = get.tyb_box[...]
    tables = []
    for l in range(LV):
        tables.append(mm(shift_rows(YG, FY // 2, YG * level - 8 * scalars.well_y[l]).astype(BF), tyb).astype(BF))
    finish(land.pt_level, sem.pt_level, LV)
    planes = jnp.zeros((128, 128), F32)
    for l in range(LV):
        move = shift_rows(128, 128, 32 * level - 4 * scalars.well_y[l], 32).astype(BF)
        planes += mm(move, land.pt_level[l])
    for p in range(PG):
        for k in range(2):
            part = planes[32 * p : 32 * (p + 1), ZP * k : ZP * (k + 1)]
            cot[pl.ds(PG * k + p, 32, stride=2 * PG), :] += part
    finish(land.q, sem.q_level, LV)

    q = land.q[...].reshape(LV * WD, 128)[:, :64]
    odd = jnp.bitwise_and(lax.broadcasted_iota(jnp.int32, q.shape, 0), 1) == 1
    q = jnp.concatenate([jnp.where(odd, 0.0, q), jnp.where(odd, q, 0.0)], axis=1).astype(BF)
    g = mm(q, get.dd_box[...]).astype(BF)
    total = jnp.zeros((YG, PG * ZP), F32)
    for l in range(LV):
        part = g[WD * l : WD * (l + 1)]
        part = jnp.concatenate([part[:, PG * ZP * k : PG * ZP * (k + 1)] for k in range(4)], axis=0)
        total += mm(tables[l], part)
    for p in range(PG):
        cot[pl.ds(p, YG, stride=PG), :] += total[:, ZP * p : ZP * (p + 1)]
    wide_cot = mm_split(cot[...], ones_cl)
    zf = get.zf_g[...]
    for b in range(NB):
        gp = (scr.slope[b].astype(F32) * (wide_cot * ro_gl[b])).astype(BF)
        put_block(scr.a, gp, b, zf)
    send_g = scr.send_g
    send_g[...] = forward_tail(scr.a, get.tyf_g[...], get.perm_out[...]).astype(BF).reshape(send_g.shape)
    push_level(lambda peer: send_g.at[peer], land.out_level, sem.out_level)
    land.out_level[level] = send_g[level]
    msg = scr.msg_out
    msg[...] = jnp.zeros(msg.shape, F32)
    for y in range(YG):
        scr.out_g[:, GZ * y : GZ * (y + 1)] = scr.pred_g[PG * y : PG * (y + 1), :GZ]
    res.coarse[...] = scr.out_g[...].astype(BF)
    for y in range(FY):
        scr.out_f[:, FZ * y : FZ * (y + 1)] = scr.pred_f[PF * y : PF * (y + 1), :]
    res.fine[0] = scr.out_f[...].astype(BF)
    finish(land.out_level, sem.out_level, LV)
    out = land.out_level
    total = out[0].astype(F32) + out[1].astype(F32) + out[2].astype(F32) + out[3].astype(F32)
    for q in range(8):
        msg[:, q, :, : 2 * CH] = total[:, 2 * CH * q : 2 * CH * (q + 1)].reshape(8, 8, 2 * CH)
    msg_ob = scr.msg_ob
    msg_ob[...] = msg[...].astype(BF)
    push_wide(lambda peer: msg_ob.at[peer // 8, peer % 8], res.got_g, sem.got_g)
    res.got_g[wide] = msg_ob[wide // 8, wide % 8]
    copies = []
    tile_out = get.tile_out[...]
    for k in range(2):
        buf = scr.gf.at[pl.ds(4 * k, 4)]
        d = scr.dual_f[:, 256 * k : 256 * (k + 1)]
        part = scr.s_f[:, 4 * CH * k : 4 * CH * (k + 1)]
        grads(part, stack_modes(d[: 2 * KF], 4, lane_f), stack_modes(d[2 * KF :], 4, lane_f), 4, spread, tile_out, buf)
        copies.append(pltpu.make_async_copy(buf, res.grad_f.at[pl.ds(4 * k, 4)], sem.out.at[k]))
        copies[-1].start()
    finish(res.got_g, sem.got_g, WD)
    for copy in copies:
        copy.wait()


def last_body(scalars, start, get, res, scr, sem):
    ins, outs = [], []
    for k in range(4):
        part = pl.ds(2 * k, 2)
        ins.append(pltpu.make_async_copy(get.grad_f.at[part], scr.buf.at[part], scr.sem_in.at[k]))
        outs.append(pltpu.make_async_copy(scr.buf.at[part], res.grad_f.at[part], scr.sem_out.at[k]))
        ins[k].start()
    start(None)
    for k in range(4):
        ins[k].wait()
        outs[k].start()
    rows = 2 * KF
    z = mm(get.txd_g[...], get.got_g[...].astype(F32).reshape(2 * GX, 128).astype(BF))
    za, zb = stack_modes(z[:rows], 2, lane_f), stack_modes(z[rows:], 2, lane_f)
    grads(get.s_g[...], za, zb, 2, get.spread, get.tile_out[...], res.grad_g)
    res.coarse[...] = get.coarse[...]
    res.fine[...] = get.fine[...]
    for copy in outs:
        copy.wait()


CHAIN_TABLES = dict(
    z4_f=Z4_F, tya_f=TYA_F, z4_g=Z4_G, tya_g=TYA_G,
    tile=TILE_CL, spread=SPREAD_IN, fold=FOLD, txs_g=TXS_G, txb_g=TXB_G, txs_f=TXS_F,
    ones_cl=ONES_CL, perm_in=PERM_WIDE, tyi_g=TYI_G, zi_g=ZI_G, sum_cl=SUM_CL, zc=ZC,
    tya_box=TYA_BOX, txs_box=TXS_BOX, txb_f=TXB_F, rows_up=ROWS_UP, z_up=Z_UP, tyi_f=TYI_F,
    zi_f=ZI_F, zf_f=ZF_F, tyf_f=TYF_F, perm_wide=PERM_WIDE_OUT, rows_down=ROWS_DOWN, z_down=Z_DOWN,
    txd_f=TXD_F, txb_box=TXB_BOX, tyb_box=TYB_BOX, dd_box=DD_BOX, zf_g=ZF_G, tyf_g=TYF_G,
    perm_out=PERM_OUT, tile_out=TILE_OUT,
)

def shards(coarse_input, fine_input, coarse_cotangent, fine_cotangent, well_x, well_y, coarse_lift, coarse_mixing,
           coarse_spectral, coarse_readout, fine_lift, fine_mixing, fine_spectral, fine_readout):
    tables = {n: jnp.asarray(t) for n, t in CHAIN_TABLES.items()}
    first = [n for n in tables][:4]
    inputs = dict(
        x_in_f=fine_input[0], x_in_g=coarse_input, **{n: tables.pop(n) for n in first},
        lift_g=coarse_lift, lift_f=fine_lift[0], mix_g=coarse_mixing, mix_f=fine_mixing[0], ro_g=coarse_readout[None],
        ro_f=fine_readout, w_f=fine_spectral[0], w_g=coarse_spectral, cot_in_f=fine_cotangent[0],
        cot_in_g=coarse_cotangent, **tables)
    scratch = {**{n + LANDED: v for n, v in LANDS.items()}, **SCRATCH}
    res = run(chain_body, RESULTS, dict(well_x=well_x, well_y=well_y), inputs, scratch, SEMS, kept=1, cid=1, name="chain")
    inputs = dict(
        grad_f=res.grad_f, got_g=res.got_g, s_g=res.s_g, spread=jnp.asarray(SPREAD_IN), tile_out=jnp.asarray(TILE_OUT),
        txd_g=jnp.asarray(TXD_G), coarse=res.coarse, fine=res.fine)
    out = run(
        last_body,
        dict(grad_f=((8, KF, 2, CC), F32), grad_g=((2, KF, 2, CC), F32), coarse=((PG, YG * GZ), BF),
             fine=((1, PF, FY * FZ), BF)),
        {}, inputs, dict(buf=((8, KF, 2, CC), F32), sem_in=4, sem_out=4), kept=1, passed=list(inputs)[:1], name="last")
    return out.coarse, out.fine, out.grad_g, out.grad_f[None]


def solution(mesh):
    placed = (
        P("wide", "level"),
        P("level", "wide", None),
        P("wide", "level"),
        P("level", "wide", None),
        P(),
        P(),
        P(),
        P(),
        P(("level", "wide"), None, None, None),
        P(),
        P("level", None, None),
        P("level", None, None),
        P("level", "wide", None, None, None),
        P("level", None),
    )
    return jax.shard_map(
        shards,
        mesh=mesh,
        in_specs=placed,
        out_specs=(
            P("wide", "level"),
            P("level", "wide", None),
            P(("level", "wide"), None, None, None),
            P("level", "wide", None, None, None),
        ),
        check_vma=False,
    )
```
